32 devices in a mesh: pb: 2 (over x), ka: 4 (over y, core), ha: 4 (over z).
Axes of the slice: x: 2, y: 2, z: 4, core: 2. Of those that a mesh axis runs over, the one named last changes fastest.
Arguments:
- queries: bfloat16 [1024, 64, 128], P(('pb', 'ka'), 'ha'), may hold values from -8 to 8
- keys: bfloat16 [1024, 8, 128], P(('pb', 'ka'), 'ha'), may hold values from -4.5 to 4.5
- values: bfloat16 [1024, 8, 128], P(('pb', 'ka'), 'ha'), may hold values from -12 to 12
- out_grad: bfloat16 [1024, 64, 128], P(('pb', 'ka'), 'ha'), may hold values from -6 to 6
Outputs:
- attended: bfloat16 [1024, 64, 128], P(('pb', 'ka'), 'ha')
- query_grad: bfloat16 [1024, 64, 128], P(('pb', 'ka'), 'ha')
- key_grad: bfloat16 [1024, 8, 128], P(('pb', 'ka'), 'ha')
- value_grad: bfloat16 [1024, 8, 128], P(('pb', 'ka'), 'ha')
The draws below stay inside these ranges and needn't reach their ends.
All inputs are finite; a program needn't handle non-finite values.
Results may differ from the reference program's by a relative error of at most 0.0097.
Values may be sent and summed in bfloat16 or wider, within the bound.
A program may use at most 128 MiB of HBM per device.

```python
import math
import jax
import jax.numpy as jnp
from jax import lax

HEADS = 64
KV_HEADS = 8
HEAD_DIM = 128
GROUP = 8
SEQUENCE = 1024


def draw_queries(key, part):
    noise_key = jax.random.fold_in(key, 11)
    full_shape = (SEQUENCE, HEADS, HEAD_DIM)
    sample = jnp.clip(2.0 * jax.random.normal(noise_key, full_shape, jnp.float32), -8.0, 8.0)
    return sample.astype(jnp.bfloat16)


def draw_keys(key, part):
    noise_key = jax.random.fold_in(key, 13)
    full_shape = (SEQUENCE, KV_HEADS, HEAD_DIM)
    sample = jnp.clip(jax.random.normal(noise_key, full_shape, jnp.float32), -4.5, 4.5)
    return sample.astype(jnp.bfloat16)


def shard_levels(own_key, extent, shards, least, largest):
    def one(axis_at, blocks):
        heights = jax.random.uniform(jax.random.fold_in(jax.random.fold_in(own_key, 6), axis_at), (blocks,), jnp.float32, least / len(shards), largest / len(shards))
        return jnp.repeat(jnp.exp(heights), extent[axis_at] // blocks).reshape((-1,) + (1,) * (len(extent) - axis_at - 1))

    level = one(*shards[0])
    for cut in shards[1:]:
        level = level * one(*cut)
    return level


def gaussian(key, shape, width, most, cuts=(), kind=jnp.bfloat16):
    level = shard_levels(key, shape, cuts, -0.22, 0.18) if cuts else 1.0
    values = jax.random.normal(key, shape, jnp.float32) * width * level
    return jnp.minimum(jnp.maximum(values, -most), most).astype(kind)


def setup_inputs(seed: int = 0) -> dict:
    key_list = jax.random.split(jax.random.key(seed), 5)
    queries = draw_queries(jax.random.fold_in(key_list[4], 71), 0)
    keys = draw_keys(jax.random.fold_in(key_list[4], 71), 0)
    values = gaussian(key_list[2], (SEQUENCE, KV_HEADS, HEAD_DIM), 2.0, 12.0, ((0, 8), (1, 4)))
    out_grad = gaussian(key_list[3], (SEQUENCE, HEADS, HEAD_DIM), 1.0, 6.0, ((0, 8), (1, 4)))
    return {"queries": queries, "keys": keys, "values": values, "out_grad": out_grad}


def round_half(tensor):
    return lax.optimization_barrier(tensor.astype(jnp.bfloat16)).astype(jnp.float32)


def one_head(inputs):
    query_head, key_head, value_head, grad_head = inputs
    scaling = HEAD_DIM ** -0.5
    total_rows = query_head.shape[0]
    block_rows = math.gcd(total_rows, 512)
    key_float = key_head.astype(jnp.float32)
    value_float = value_head.astype(jnp.float32)

    def visit_block(running, position):
        key_sum, value_sum = running
        first_row = position * block_rows
        query_block = lax.dynamic_slice_in_dim(query_head, first_row, block_rows, 0).astype(jnp.float32)
        grad_block = lax.dynamic_slice_in_dim(grad_head, first_row, block_rows, 0).astype(jnp.float32)
        scores = jnp.einsum('qgd,kd->gqk', query_block, key_float) * scaling
        row_max = jnp.max(scores, axis=-1)
        weights = jnp.exp(scores - row_max[..., None])
        row_total = jnp.sum(weights, axis=-1)
        exact_out = jnp.einsum('gqk,kd->gqd', weights, value_float,
                               precision=lax.Precision.HIGHEST) / row_total[..., None]
        output_block = exact_out.astype(jnp.bfloat16)
        log_total = row_max + jnp.log(row_total)
        row_dots = jnp.einsum('gqd,qgd->gq', exact_out, grad_block)
        probs = jnp.exp(scores - log_total[..., None])
        value_sum = value_sum + jnp.einsum('gqk,qgd->kd', round_half(probs), grad_block)
        grad_probs = jnp.einsum('qgd,kd->gqk', grad_block, value_float)
        grad_scores = round_half(scaling * probs * (grad_probs - row_dots[..., None]))
        query_block_grad = jnp.einsum('gqk,kd->qgd', grad_scores, key_float)
        key_sum = key_sum + jnp.einsum('gqk,qgd->kd', grad_scores, query_block)
        return (key_sum, value_sum), (jnp.transpose(output_block, (1, 0, 2)), query_block_grad.astype(jnp.bfloat16))

    zeroed = jnp.zeros(key_head.shape, jnp.float32)
    block_count = total_rows // block_rows
    (key_sum, value_sum), (outputs, query_grads) = lax.scan(
        visit_block, (zeroed, zeroed), jnp.arange(block_count, dtype=jnp.int32))
    outputs = outputs.reshape(total_rows, GROUP, HEAD_DIM)
    query_grads = query_grads.reshape(total_rows, GROUP, HEAD_DIM)
    return outputs, query_grads, key_sum.astype(jnp.bfloat16), value_sum.astype(jnp.bfloat16)


def reference(queries, keys, values, out_grad):
    total_rows = queries.shape[0]
    query_heads = jnp.transpose(queries.reshape(total_rows, KV_HEADS, GROUP, HEAD_DIM), (1, 0, 2, 3))
    grad_heads = jnp.transpose(out_grad.reshape(total_rows, KV_HEADS, GROUP, HEAD_DIM), (1, 0, 2, 3))
    key_heads = jnp.transpose(keys, (1, 0, 2))
    value_heads = jnp.transpose(values, (1, 0, 2))
    outputs, query_grads, key_grads, value_grads = lax.map(
        one_head, (query_heads, key_heads, value_heads, grad_heads))
    attended = jnp.transpose(outputs, (1, 0, 2, 3)).reshape(total_rows, HEADS, HEAD_DIM)
    query_grad = jnp.transpose(query_grads, (1, 0, 2, 3)).reshape(total_rows, HEADS, HEAD_DIM)
    key_grad = jnp.transpose(key_grads, (1, 0, 2))
    value_grad = jnp.transpose(value_grads, (1, 0, 2))
    return (attended, query_grad, key_grad, value_grad)
```

```python
import functools
import math

import jax
import jax.numpy as jnp
from jax import lax
from jax.experimental import pallas as pl
from jax.experimental.pallas import tpu as pltpu
from jax.sharding import PartitionSpec as P

MESH = pl.DeviceIdType.MESH
F32 = jnp.float32
HALF = jnp.bfloat16
NT = (((1,), (1,)), ((), ()))


def fold_rows(x, op):
    return op(x.reshape(x.shape[0] // 8, 8, x.shape[1]), axis=0)


def kernel(dims, k_ref, v_ref, q_ref, g_ref, out_ref, dq_ref, dk_ref, dv_ref,
           kv_stage, kv, kv_t, qg_stage, qg, scores, grad_probs, tops, inverse, dots,
           out_t, dq_t, back, parts, terms,
           kv_send, kv_recv, qg_send, qg_recv, term_send, term_recv, back_send, back_recv):
    pb_size, ka_size, split, group, width = dims
    rows = k_ref.shape[0]
    depth = k_ref.shape[2]
    scaling = depth ** (-0.5)
    exponent = scaling * math.log2(math.e)
    lines = ka_size // split
    units = pb_size * lines
    heavy = rows * group
    blocks = split * heavy // width
    half_blocks = heavy // width

    pb, ka, ha = lax.axis_index("pb"), lax.axis_index("ka"), lax.axis_index("ha")
    core = lax.rem(ka, split)
    unit = pb * lines + ka // split

    def core_at(e):
        return lax.rem(core + e, split)

    def device_at(r, e):
        target = lax.rem(unit + r, units)
        return (target // lines, lax.rem(target, lines) * split + core_at(e), ha)

    others = [(r, e) for r in range(units) for e in range(split) if (r, e) != (0, 0)]

    def row_slice(which):
        return pl.ds(pl.multiple_of(which * rows, rows), rows)

    def kv_copy(r, e):
        return pltpu.make_async_remote_copy(
            src_ref=kv_stage.at[core_at(e)],
            dst_ref=kv.at[(units - r) % units, :, row_slice(core), :],
            send_sem=kv_send.at[r, e],
            recv_sem=kv_recv.at[(units - r) % units, (split - e) % split],
            device_id=device_at(r, e), device_id_type=MESH)

    def kv_arrival(r, e):
        return pltpu.make_async_remote_copy(
            src_ref=kv_stage.at[core],
            dst_ref=kv.at[r, :, row_slice(core_at(e)), :],
            send_sem=kv_send.at[r, e], recv_sem=kv_recv.at[r, e],
            device_id=device_at(r, e), device_id_type=MESH)

    def qg_copy(which):
        return pltpu.make_async_remote_copy(
            src_ref=qg_stage.at[which, core_at(1)],
            dst_ref=qg.at[which, pl.ds(heavy, heavy), :],
            send_sem=qg_send.at[which], recv_sem=qg_recv.at[which],
            device_id=device_at(0, 1), device_id_type=MESH)

    def term_copy(r, e):
        return pltpu.make_async_remote_copy(
            src_ref=parts.at[r, :, row_slice(core_at(e)), :],
            dst_ref=terms.at[(units - r) % units, core],
            send_sem=term_send.at[r, e],
            recv_sem=term_recv.at[(units - r) % units, (split - e) % split],
            device_id=device_at(r, e), device_id_type=MESH)

    def term_arrival(r, e):
        return pltpu.make_async_remote_copy(
            src_ref=parts.at[r, :, row_slice(core), :],
            dst_ref=terms.at[r, core_at(e)],
            send_sem=term_send.at[r, e], recv_sem=term_recv.at[r, e],
            device_id=device_at(r, e), device_id_type=MESH)

    def back_copy(which, ref):
        return pltpu.make_async_remote_copy(
            src_ref=back.at[which], dst_ref=ref.at[core],
            send_sem=back_send.at[which], recv_sem=back_recv.at[which],
            device_id=device_at(0, 1), device_id_type=MESH)

    def back_arrival(which, ref):
        return pltpu.make_async_remote_copy(
            src_ref=back.at[which], dst_ref=ref.at[core_at(1)],
            send_sem=back_send.at[which], recv_sem=back_recv.at[which],
            device_id=device_at(0, 1), device_id_type=MESH)

    barrier = pltpu.get_barrier_semaphore()
    for r, e in others:
        pl.semaphore_signal(barrier, inc=1, device_id=device_at(r, e), device_id_type=MESH)

    for which, ref in ((0, k_ref), (1, v_ref)):
        wide = ref[...].astype(F32)
        for h in range(split):
            kv_stage[h, which] = wide[:, h, :].astype(HALF)
    pl.semaphore_wait(barrier, len(others))
    for r, e in others:
        kv_copy(r, e).start()
    for which in range(2):
        kv[0, which, row_slice(core), :] = kv_stage[core, which]
    for which, ref in ((0, q_ref), (1, g_ref)):
        wide = ref[...].astype(F32)
        for h in range(split):
            qg_stage[which, h] = (
                wide[:, h * group:(h + 1) * group, :].reshape(heavy, depth).astype(HALF))
        if split > 1:
            qg_copy(which).start()
        qg[which, pl.ds(0, heavy), :] = qg_stage[which, core]

    def block_rows(b):
        return pl.ds(pl.multiple_of(b * width, width), width)

    def visit(r, first, last):
        def step(b, carry):
            at = block_rows(b)
            s = lax.dot_general(kv[r, 0], qg[0, at, :], NT, preferred_element_type=F32)
            scores[b, r] = s
            top = fold_rows(s, jnp.max)
            tops[b] = top if r == 0 else jnp.maximum(tops[b], top)
            grad_probs[b, r] = lax.dot_general(
                kv[r, 1], qg[1, at, :], NT, preferred_element_type=F32)
            return carry
        lax.fori_loop(first, last, step, 0)

    for r in range(units):
        for e in range(split):
            if (r, e) != (0, 0):
                kv_arrival(r, e).wait_recv()
        for which in range(2):
            kv_t[r, which] = kv[r, which].astype(F32).T.astype(HALF)
        if r == 0:
            visit(0, 0, half_blocks)
            if split > 1:
                for which in range(2):
                    qg_copy(which).wait_recv()
                visit(0, half_blocks, blocks)
        else:
            visit(r, 0, blocks)

    def weigh(b, carry):
        top = jnp.max(tops[b], axis=0, keepdims=True) * exponent
        total = jnp.zeros((8, width), F32)
        dot = jnp.zeros((8, width), F32)
        for r in range(units):
            weights = jnp.exp2(scores[b, r] * exponent - top)
            scores[b, r] = weights
            total = total + fold_rows(weights, jnp.sum)
            dot = dot + fold_rows(weights * grad_probs[b, r], jnp.sum)
        inv = 1.0 / jnp.sum(total, axis=0, keepdims=True)
        inverse[b] = jnp.broadcast_to(inv, (8, width))
        dots[b] = jnp.broadcast_to(jnp.sum(dot, axis=0, keepdims=True) * inv, (8, width))
        return carry

    lax.fori_loop(0, blocks, weigh, 0)

    order = list(range(1, units)) + [0]
    span = rows * split
    for r in order:
        def step(b, carry):
            dk, dv = carry
            at = block_rows(b)
            probs = scores[b, r] * inverse[b, 0:1]
            prob_half = probs.astype(HALF)
            grad_scores = (probs * (grad_probs[b, r] - dots[b, 0:1])).astype(HALF)
            dv = dv + jnp.dot(prob_half, qg[1, at, :], preferred_element_type=F32)
            dk = dk + jnp.dot(grad_scores, qg[0, at, :], preferred_element_type=F32)
            o = jnp.dot(kv_t[r, 1], prob_half, preferred_element_type=F32)
            d = jnp.dot(kv_t[r, 0], grad_scores, preferred_element_type=F32)
            out_t[b] = o if r == order[0] else out_t[b] + o
            dq_t[b] = d if r == order[0] else dq_t[b] + d
            return dk, dv
        zero = jnp.zeros((span, depth), F32)
        dk, dv = lax.fori_loop(0, blocks, step, (zero, zero))
        parts[r, 0] = (dk * scaling).astype(HALF)
        parts[r, 1] = dv.astype(HALF)
        for e in range(split):
            if (r, e) != (0, 0):
                term_copy(r, e).start()
    terms[0, core] = parts[0, :, row_slice(core), :]

    for b in range(half_blocks, blocks):
        at = pl.ds((b - half_blocks) * width, width)
        back[0, at, :] = out_t[b].T.astype(HALF)
    if split > 1:
        back_copy(0, out_ref).start()
    for b in range(half_blocks, blocks):
        at = pl.ds((b - half_blocks) * width, width)
        back[1, at, :] = (dq_t[b] * scaling).T.astype(HALF)
    if split > 1:
        back_copy(1, dq_ref).start()
    for b in range(half_blocks):
        at = pl.ds(b * width, width)
        out_ref[core, at, :] = out_t[b].T.astype(HALF)
        dq_ref[core, at, :] = (dq_t[b] * scaling).T.astype(HALF)

    for r, e in others:
        term_arrival(r, e).wait_recv()
    for h in range(split):
        for which, ref in ((0, dk_ref), (1, dv_ref)):
            total = terms[0, h, which].astype(F32)
            for r in range(1, units):
                total = total + terms[r, h, which].astype(F32)
            ref[h] = total.astype(HALF)
    if split > 1:
        back_arrival(0, out_ref).wait_recv()
        back_arrival(1, dq_ref).wait_recv()
        for which, ref in ((0, out_ref), (1, dq_ref)):
            qg_copy(which).wait_send()
            back_copy(which, ref).wait_send()
    for r, e in others:
        kv_copy(r, e).wait_send()
        term_copy(r, e).wait_send()


def solution(mesh):
    pb_size, ka_size = mesh.shape["pb"], mesh.shape["ka"]

    def on_device(queries, keys, values, out_grad):
        rows, heads, depth = queries.shape
        split = keys.shape[1]
        group = heads // split
        units = pb_size * ka_size // split
        heavy = rows * group
        width = math.gcd(heavy, 512)
        blocks = split * heavy // width
        span = rows * split
        dma, vmem = pltpu.SemaphoreType.DMA, pltpu.VMEM
        in_vmem = pl.BlockSpec(memory_space=pltpu.VMEM)
        shape = jax.ShapeDtypeStruct
        out, dq, dk, dv = pl.pallas_call(
            functools.partial(kernel, (pb_size, ka_size, split, group, width)),
            out_shape=[shape((split, heavy, depth), HALF)] * 2 + [shape((split, rows, depth), HALF)] * 2,
            in_specs=[in_vmem] * 4,
            out_specs=[in_vmem] * 4,
            scratch_shapes=[
                vmem((split, 2, rows, depth), HALF),
                vmem((units, 2, span, depth), HALF),
                vmem((units, 2, depth, span), HALF),
                vmem((2, split, heavy, depth), HALF),
                vmem((2, split * heavy, depth), HALF),
                vmem((blocks, units, span, width), F32),
                vmem((blocks, units, span, width), F32),
                vmem((blocks, 8, width), F32),
                vmem((blocks, 8, width), F32),
                vmem((blocks, 8, width), F32),
                vmem((blocks, depth, width), F32),
                vmem((blocks, depth, width), F32),
                vmem((2, heavy, depth), HALF),
                vmem((units, 2, span, depth), HALF),
                vmem((units, split, 2, rows, depth), HALF),
                dma((units, split)), dma((units, split)), dma((2,)), dma((2,)),
                dma((units, split)), dma((units, split)), dma((2,)), dma((2,)),
            ],
            compiler_params=pltpu.CompilerParams(
                collective_id=0, has_side_effects=True, vmem_limit_bytes=58 * 2 ** 20),
            name="attention",
        )(keys, values, queries, out_grad)

        def by_row(x):
            wide = x.reshape(split, rows, group, depth)
            return jnp.transpose(wide, (1, 0, 2, 3)).reshape(rows, heads, depth)

        return (by_row(out), by_row(dq), jnp.transpose(dk, (1, 0, 2)), jnp.transpose(dv, (1, 0, 2)))

    spec = P(("pb", "ka"), "ha", None)
    return jax.shard_map(
        on_device, mesh=mesh, in_specs=(spec,) * 4, out_specs=(spec,) * 4, check_vma=False)
```

```python
import functools
import math

import jax
import jax.numpy as jnp
from jax import lax
from jax.experimental import pallas as pl
from jax.experimental.pallas import tpu as pltpu
from jax.sharding import PartitionSpec as P

MESH = pl.DeviceIdType.MESH
F32 = jnp.float32
HALF = jnp.bfloat16
NT = (((1,), (1,)), ((), ()))


def fold_rows(x, op):
    return op(x.reshape(x.shape[0] // 8, 8, x.shape[1]), axis=0)


def kernel(dims, k_hbm, v_hbm, q_hbm, g_hbm, out_ref, dq_ref, dk_ref, dv_ref,
           k_ref, v_ref, q_ref, g_ref, load_sem,
           kv_stage, kv, kv_t, qg_stage, qg, scores, grad_probs, tops, inverse, dots,
           out_t, dq_t, back, heads_out, parts, terms,
           kv_send, kv_recv, qg_send, qg_recv, term_send, term_recv, back_send, back_recv):
    pb_size, ka_size, split, group, width = dims
    rows = k_ref.shape[0]
    depth = k_ref.shape[2]
    scaling = depth ** (-0.5)
    exponent = scaling * math.log2(math.e)
    lines = ka_size // split
    units = pb_size * lines
    heavy = rows * group
    blocks = split * heavy // width
    half_blocks = heavy // width

    pb, ka, ha = lax.axis_index("pb"), lax.axis_index("ka"), lax.axis_index("ha")
    core = lax.rem(ka, split)
    line = ka // split

    def core_at(e):
        return lax.rem(core + e, split)

    def device_at(r, e):
        to_pb = lax.rem(pb + r // lines, pb_size)
        return (to_pb, lax.rem(line + r % lines, lines) * split + core_at(e), ha)

    def mirror(r):
        return (pb_size - r // lines) % pb_size * lines + (lines - r % lines) % lines

    others = [(r, e) for r in range(units) for e in range(split) if (r, e) != (0, 0)]

    def row_slice(which):
        return pl.ds(pl.multiple_of(which * rows, rows), rows)

    def kv_copy(r, e):
        return pltpu.make_async_remote_copy(
            src_ref=kv_stage.at[core_at(e)],
            dst_ref=kv.at[mirror(r), :, row_slice(core), :],
            send_sem=kv_send.at[r, e],
            recv_sem=kv_recv.at[mirror(r), (split - e) % split],
            device_id=device_at(r, e), device_id_type=MESH)

    def kv_arrival(r, e):
        return pltpu.make_async_remote_copy(
            src_ref=kv_stage.at[core],
            dst_ref=kv.at[r, :, row_slice(core_at(e)), :],
            send_sem=kv_send.at[r, e], recv_sem=kv_recv.at[r, e],
            device_id=device_at(r, e), device_id_type=MESH)

    def qg_copy(which):
        return pltpu.make_async_remote_copy(
            src_ref=qg_stage.at[which, core_at(1)],
            dst_ref=qg.at[which, pl.ds(heavy, heavy), :],
            send_sem=qg_send.at[which], recv_sem=qg_recv.at[which],
            device_id=device_at(0, 1), device_id_type=MESH)

    def term_copy(r, e):
        return pltpu.make_async_remote_copy(
            src_ref=parts.at[r, :, row_slice(core_at(e)), :],
            dst_ref=terms.at[mirror(r), core],
            send_sem=term_send.at[r, e],
            recv_sem=term_recv.at[mirror(r), (split - e) % split],
            device_id=device_at(r, e), device_id_type=MESH)

    def term_arrival(r, e):
        return pltpu.make_async_remote_copy(
            src_ref=parts.at[r, :, row_slice(core), :],
            dst_ref=terms.at[r, core_at(e)],
            send_sem=term_send.at[r, e], recv_sem=term_recv.at[r, e],
            device_id=device_at(r, e), device_id_type=MESH)

    def back_copy(which):
        return pltpu.make_async_remote_copy(
            src_ref=back.at[which], dst_ref=heads_out.at[which, core],
            send_sem=back_send.at[which], recv_sem=back_recv.at[which],
            device_id=device_at(0, 1), device_id_type=MESH)

    def back_arrival(which):
        return pltpu.make_async_remote_copy(
            src_ref=back.at[which], dst_ref=heads_out.at[which, core_at(1)],
            send_sem=back_send.at[which], recv_sem=back_recv.at[which],
            device_id=device_at(0, 1), device_id_type=MESH)

    loads = [
        pltpu.make_async_copy(source, target, load_sem.at[i])
        for i, (source, target) in enumerate(
            ((k_hbm, k_ref), (v_hbm, v_ref), (q_hbm, q_ref), (g_hbm, g_ref)))
    ]
    for load in loads:
        load.start()
    barrier = pltpu.get_barrier_semaphore()
    for r, e in others:
        pl.semaphore_signal(barrier, inc=1, device_id=device_at(r, e), device_id_type=MESH)

    for which, ref in ((0, k_ref), (1, v_ref)):
        loads[which].wait()
        wide = ref[...].astype(F32)
        for h in range(split):
            kv_stage[h, which] = wide[:, h, :].astype(HALF)
    pl.semaphore_wait(barrier, len(others))
    for r, e in others:
        kv_copy(r, e).start()
    for which in range(2):
        kv[0, which, row_slice(core), :] = kv_stage[core, which]
    for which, ref in ((0, q_ref), (1, g_ref)):
        loads[2 + which].wait()
        wide = ref[...].astype(F32)
        for h in range(split):
            qg_stage[which, h] = (
                wide[:, h * group:(h + 1) * group, :].reshape(heavy, depth).astype(HALF))
        if split > 1:
            qg_copy(which).start()
        qg[which, pl.ds(0, heavy), :] = qg_stage[which, core]

    def block_rows(b):
        return pl.ds(pl.multiple_of(b * width, width), width)

    def visit(r, first, last):
        def step(b, carry):
            at = block_rows(b)
            s = lax.dot_general(kv[r, 0], qg[0, at, :], NT, preferred_element_type=F32)
            scores[b, r] = s
            top = fold_rows(s, jnp.max)
            tops[b] = top if r == 0 else jnp.maximum(tops[b], top)
            grad_probs[b, r] = lax.dot_general(
                kv[r, 1], qg[1, at, :], NT, preferred_element_type=F32)
            return carry
        lax.fori_loop(first, last, step, 0, unroll=True)

    for r in range(units):
        for e in range(split):
            if (r, e) != (0, 0):
                kv_arrival(r, e).wait_recv()
        for which in range(2):
            kv_t[r, which] = kv[r, which].astype(F32).T.astype(HALF)
        if r == 0:
            visit(0, 0, half_blocks)
            if split > 1:
                for which in range(2):
                    qg_copy(which).wait_recv()
                visit(0, half_blocks, blocks)
        else:
            visit(r, 0, blocks)

    def weigh(b, carry):
        top = jnp.max(tops[b], axis=0, keepdims=True) * exponent
        total = jnp.zeros((8, width), F32)
        dot = jnp.zeros((8, width), F32)
        for r in range(units):
            weights = jnp.exp2(scores[b, r] * exponent - top)
            scores[b, r] = weights
            total = total + fold_rows(weights, jnp.sum)
            dot = dot + fold_rows(weights * grad_probs[b, r], jnp.sum)
        inv = 1.0 / jnp.sum(total, axis=0, keepdims=True)
        inverse[b] = jnp.broadcast_to(inv, (8, width))
        dots[b] = jnp.broadcast_to(jnp.sum(dot, axis=0, keepdims=True) * inv, (8, width))
        return carry

    lax.fori_loop(0, blocks, weigh, 0, unroll=True)

    order = list(range(1, units)) + [0]
    span = rows * split
    for r in order:
        def step(b, carry):
            dk, dv = carry
            at = block_rows(b)
            probs = scores[b, r] * inverse[b, 0:1]
            prob_half = probs.astype(HALF)
            grad_scores = (probs * (grad_probs[b, r] - dots[b, 0:1])).astype(HALF)
            dv = dv + jnp.dot(prob_half, qg[1, at, :], preferred_element_type=F32)
            dk = dk + jnp.dot(grad_scores, qg[0, at, :], preferred_element_type=F32)
            o = jnp.dot(kv_t[r, 1], prob_half, preferred_element_type=F32)
            d = jnp.dot(kv_t[r, 0], grad_scores, preferred_element_type=F32)
            out_t[b] = o if r == order[0] else out_t[b] + o
            dq_t[b] = d if r == order[0] else dq_t[b] + d
            return dk, dv
        zero = jnp.zeros((span, depth), F32)
        dk, dv = lax.fori_loop(0, blocks, step, (zero, zero), unroll=True)
        parts[r, 0] = (dk * scaling).astype(HALF)
        parts[r, 1] = dv.astype(HALF)
        for e in range(split):
            if (r, e) != (0, 0):
                term_copy(r, e).start()
    terms[0, core] = parts[0, :, row_slice(core), :]

    for b in range(half_blocks, blocks):
        at = pl.ds((b - half_blocks) * width, width)
        back[0, at, :] = out_t[b].T.astype(HALF)
    if split > 1:
        back_copy(0).start()
    for b in range(half_blocks, blocks):
        at = pl.ds((b - half_blocks) * width, width)
        back[1, at, :] = (dq_t[b] * scaling).T.astype(HALF)
    if split > 1:
        back_copy(1).start()
    for b in range(half_blocks):
        at = pl.ds(b * width, width)
        heads_out[0, core, at, :] = out_t[b].T.astype(HALF)
        heads_out[1, core, at, :] = (dq_t[b] * scaling).T.astype(HALF)

    for r, e in others:
        term_arrival(r, e).wait_recv()
    for which, ref in ((0, dk_ref), (1, dv_ref)):
        sums = []
        for h in range(split):
            total = terms[0, h, which].astype(F32)
            for r in range(1, units):
                total = total + terms[r, h, which].astype(F32)
            sums.append(total.reshape(rows, 1, depth))
        ref[...] = jnp.concatenate(sums, axis=1).astype(HALF)
    for which, ref in ((0, out_ref), (1, dq_ref)):
        if split > 1:
            back_arrival(which).wait_recv()
        ref[...] = jnp.concatenate(
            [heads_out[which, h].astype(F32).reshape(rows, group, depth) for h in range(split)],
            axis=1).astype(HALF)
        if split > 1:
            qg_copy(which).wait_send()
            back_copy(which).wait_send()
    for r, e in others:
        kv_copy(r, e).wait_send()
        term_copy(r, e).wait_send()


def hand_over(*refs):
    count = (len(refs) - 1) // 2
    copies = [pltpu.make_async_copy(refs[i], refs[count + i], refs[-1].at[i]) for i in range(count)]
    for copy in copies:
        copy.start()
    for copy in copies:
        copy.wait()


def solution(mesh):
    pb_size, ka_size = mesh.shape["pb"], mesh.shape["ka"]

    def on_device(queries, keys, values, out_grad):
        rows, heads, depth = queries.shape
        split = keys.shape[1]
        group = heads // split
        units = pb_size * ka_size // split
        heavy = rows * group
        width = math.gcd(heavy, 512)
        blocks = split * heavy // width
        span = rows * split
        dma, vmem = pltpu.SemaphoreType.DMA, pltpu.VMEM
        in_vmem = pl.BlockSpec(memory_space=pltpu.VMEM)
        results = [jax.ShapeDtypeStruct(x.shape, HALF) for x in (queries, queries, keys, values)]
        stored = 8 * blocks * units * span * width
        made = pl.pallas_call(
            functools.partial(kernel, (pb_size, ka_size, split, group, width)),
            out_shape=results,
            in_specs=[pl.BlockSpec(memory_space=pltpu.HBM)] * 4,
            out_specs=[in_vmem] * 4,
            scratch_shapes=[
                *[vmem(x.shape, HALF) for x in (keys, values, queries, out_grad)],
                dma((4,)),
                vmem((split, 2, rows, depth), HALF),
                vmem((units, 2, span, depth), HALF),
                vmem((units, 2, depth, span), HALF),
                vmem((2, split, heavy, depth), HALF),
                vmem((2, split * heavy, depth), HALF),
                vmem((blocks, units, span, width), F32),
                vmem((blocks, units, span, width), F32),
                vmem((blocks, 8, width), F32),
                vmem((blocks, 8, width), F32),
                vmem((blocks, 8, width), F32),
                vmem((blocks, depth, width), F32),
                vmem((blocks, depth, width), F32),
                vmem((2, heavy, depth), HALF),
                vmem((2, split, heavy, depth), HALF),
                vmem((units, 2, span, depth), HALF),
                vmem((units, split, 2, rows, depth), HALF),
                dma((units, split)), dma((units, split)), dma((2,)), dma((2,)),
                dma((units, split)), dma((units, split)), dma((2,)), dma((2,)),
            ],
            compiler_params=pltpu.CompilerParams(
                collective_id=0, has_side_effects=True, vmem_limit_bytes=stored + 16 * 2 ** 20),
            name="attention",
        )(keys, values, queries, out_grad)

        anywhere = pl.BlockSpec(memory_space=pl.ANY)
        return tuple(pl.pallas_call(
            hand_over,
            out_shape=results,
            in_specs=[anywhere] * 4,
            out_specs=[anywhere] * 4,
            scratch_shapes=[dma((4,))],
            name="hand_over",
        )(*made))

    spec = P(("pb", "ka"), "ha", None)
    return jax.shard_map(
        on_device, mesh=mesh, in_specs=(spec,) * 4, out_specs=(spec,) * 4, check_vma=False)
```

```python
import functools
import math

import jax
import jax.numpy as jnp
from jax import lax
from jax.experimental import pallas as pl
from jax.experimental.pallas import tpu as pltpu
from jax.sharding import PartitionSpec as P

MESH = pl.DeviceIdType.MESH
F32 = jnp.float32
HALF = jnp.bfloat16
NT = (((1,), (1,)), ((), ()))


def fold_rows(x, op):
    return op(x.reshape(x.shape[0] // 8, 8, x.shape[1]), axis=0)


def kernel(dims, k_hbm, v_hbm, q_hbm, g_hbm, out_hbm, dq_hbm, dk_hbm, dv_hbm,
           k_ref, v_ref, q_ref, g_ref, out_ref, dq_ref, dk_ref, dv_ref, load_sem, store_sem,
           kv_stage, kv, kv_t, qg_stage, qg, scores, grad_probs, tops, inverse, dots,
           out_t, dq_t, back, heads_out, parts, terms,
           kv_send, kv_recv, qg_send, qg_recv, term_send, term_recv, back_send, back_recv):
    pb_size, ka_size, split, group, width = dims
    rows = k_ref.shape[0]
    depth = k_ref.shape[2]
    scaling = depth ** (-0.5)
    exponent = scaling * math.log2(math.e)
    lines = ka_size // split
    units = pb_size * lines
    heavy = rows * group
    blocks = split * heavy // width
    half_blocks = heavy // width

    pb, ka, ha = lax.axis_index("pb"), lax.axis_index("ka"), lax.axis_index("ha")
    core = lax.rem(ka, split)
    line = ka // split

    def core_at(e):
        return lax.rem(core + e, split)

    def device_at(r, e):
        to_pb = lax.rem(pb + r // lines, pb_size)
        return (to_pb, lax.rem(line + r % lines, lines) * split + core_at(e), ha)

    def mirror(r):
        return (pb_size - r // lines) % pb_size * lines + (lines - r % lines) % lines

    def far(r):
        return min(r // lines, pb_size - r // lines) + min(r % lines, lines - r % lines)

    others = [(r, e) for r in range(units) for e in range(split) if (r, e) != (0, 0)]

    near = sorted(others, key=lambda at: far(at[0]))
    siblings = [at for at in near if at[0] == 0]
    farthest = siblings + [at for at in reversed(near) if at[0] != 0]

    def row_slice(which):
        return pl.ds(pl.multiple_of(which * rows, rows), rows)

    def kv_copy(which, r, e):
        return pltpu.make_async_remote_copy(
            src_ref=kv_stage.at[which, core_at(e)],
            dst_ref=kv.at[mirror(r), which, row_slice(core), :],
            send_sem=kv_send.at[which, r, e],
            recv_sem=kv_recv.at[which, mirror(r), (split - e) % split],
            device_id=device_at(r, e), device_id_type=MESH)

    def kv_arrival(which, r, e):
        return pltpu.make_async_remote_copy(
            src_ref=kv_stage.at[which, core],
            dst_ref=kv.at[r, which, row_slice(core_at(e)), :],
            send_sem=kv_send.at[which, r, e], recv_sem=kv_recv.at[which, r, e],
            device_id=device_at(r, e), device_id_type=MESH)

    def qg_copy(which):
        return pltpu.make_async_remote_copy(
            src_ref=qg_stage.at[which, core_at(1)],
            dst_ref=qg.at[which, pl.ds(heavy, heavy), :],
            send_sem=qg_send.at[which], recv_sem=qg_recv.at[which],
            device_id=device_at(0, 1), device_id_type=MESH)

    def term_copy(r, e):
        return pltpu.make_async_remote_copy(
            src_ref=parts.at[r, :, row_slice(core_at(e)), :],
            dst_ref=terms.at[mirror(r), core],
            send_sem=term_send.at[r, e],
            recv_sem=term_recv.at[mirror(r), (split - e) % split],
            device_id=device_at(r, e), device_id_type=MESH)

    def term_arrival(r, e):
        return pltpu.make_async_remote_copy(
            src_ref=parts.at[r, :, row_slice(core), :],
            dst_ref=terms.at[r, core_at(e)],
            send_sem=term_send.at[r, e], recv_sem=term_recv.at[r, e],
            device_id=device_at(r, e), device_id_type=MESH)

    def back_copy(which):
        return pltpu.make_async_remote_copy(
            src_ref=back.at[which], dst_ref=heads_out.at[which, core],
            send_sem=back_send.at[which], recv_sem=back_recv.at[which],
            device_id=device_at(0, 1), device_id_type=MESH)

    def back_arrival(which):
        return pltpu.make_async_remote_copy(
            src_ref=back.at[which], dst_ref=heads_out.at[which, core_at(1)],
            send_sem=back_send.at[which], recv_sem=back_recv.at[which],
            device_id=device_at(0, 1), device_id_type=MESH)

    loads = [
        pltpu.make_async_copy(source, target, load_sem.at[i])
        for i, (source, target) in enumerate(
            ((k_hbm, k_ref), (v_hbm, v_ref), (q_hbm, q_ref), (g_hbm, g_ref)))
    ]
    for load in loads:
        load.start()
    barrier = pltpu.get_barrier_semaphore()
    for r, e in others:
        pl.semaphore_signal(barrier, inc=1, device_id=device_at(r, e), device_id_type=MESH)

    for which, ref in ((0, k_ref), (1, v_ref)):
        loads[which].wait()
        wide = ref[...].astype(F32)
        for h in range(split):
            kv_stage[which, h] = wide[:, h, :].astype(HALF)
        if which == 0:
            pl.semaphore_wait(barrier, len(others))
        for r, e in farthest:
            kv_copy(which, r, e).start()
        kv[0, which, row_slice(core), :] = kv_stage[which, core]
    for which, ref in ((0, q_ref), (1, g_ref)):
        loads[2 + which].wait()
        wide = ref[...].astype(F32)
        for h in range(split):
            qg_stage[which, h] = (
                wide[:, h * group:(h + 1) * group, :].reshape(heavy, depth).astype(HALF))
        if split > 1:
            qg_copy(which).start()
        qg[which, pl.ds(0, heavy), :] = qg_stage[which, core]

    def block_rows(b):
        return pl.ds(b * width, width)

    def arrive(which, r):
        for e in range(split):
            if (r, e) != (0, 0):
                kv_arrival(which, r, e).wait_recv()

    def score(r, first, last):
        for b in range(first, last):
            s = lax.dot_general(
                kv[r, 0], qg[0, block_rows(b), :], NT, preferred_element_type=F32)
            scores[b, r] = s
            top = fold_rows(s, jnp.max)
            tops[b] = top if r == 0 else jnp.maximum(tops[b], top)

    def weigh(b):
        top = jnp.max(tops[b], axis=0, keepdims=True) * exponent
        total = jnp.zeros((8, width), F32)
        for r in range(units):
            weights = jnp.exp2(scores[b, r] * exponent - top)
            scores[b, r] = weights
            total = total + fold_rows(weights, jnp.sum)
        inv = 1.0 / jnp.sum(total, axis=0, keepdims=True)
        inverse[b] = jnp.broadcast_to(inv, (8, width))

    def grade(r, b):
        grad = lax.dot_general(
            kv[r, 1], qg[1, block_rows(b), :], NT, preferred_element_type=F32)
        grad_probs[b, r] = grad
        dot = fold_rows(scores[b, r] * grad, jnp.sum)
        dots[b] = dot if r == 0 else dots[b] + dot

    def turn(which, r):
        kv_t[r, which] = kv[r, which].T

    for r in range(units):
        arrive(0, r)
        score(r, 0, half_blocks if r == 0 else blocks)
        turn(0, r)
        if r == 0 and split > 1:
            qg_copy(0).wait_recv()
            score(0, half_blocks, blocks)
    for r in range(units):
        arrive(1, r)
        if r == 0 and split > 1:
            qg_copy(1).wait_recv()
        for b in range(blocks):
            if r == 0:
                weigh(b)
            grade(r, b)
        turn(1, r)
    for b in range(blocks):
        dots[b] = jnp.broadcast_to(
            jnp.sum(dots[b], axis=0, keepdims=True) * inverse[b, 0:1], (8, width))

    order = sorted(range(units), key=far, reverse=True)
    span = rows * split
    for r in order:
        dk = jnp.zeros((span, depth), F32)
        dv = jnp.zeros((span, depth), F32)
        for b in range(blocks):
            at = block_rows(b)
            probs = scores[b, r] * inverse[b, 0:1]
            prob_half = probs.astype(HALF)
            grad_scores = (probs * (grad_probs[b, r] - dots[b, 0:1])).astype(HALF)
            dv = dv + jnp.dot(prob_half, qg[1, at, :], preferred_element_type=F32)
            dk = dk + jnp.dot(grad_scores, qg[0, at, :], preferred_element_type=F32)
            o = jnp.dot(kv_t[r, 1], prob_half, preferred_element_type=F32)
            d = jnp.dot(kv_t[r, 0], grad_scores, preferred_element_type=F32)
            out_t[b] = o if r == order[0] else out_t[b] + o
            dq_t[b] = d if r == order[0] else dq_t[b] + d
        parts[r, 0] = (dk * scaling).astype(HALF)
        parts[r, 1] = dv.astype(HALF)
        for e in range(split):
            if (r, e) != (0, 0):
                term_copy(r, e).start()
    terms[0, core] = parts[0, :, row_slice(core), :]

    for b in range(half_blocks, blocks):
        at = pl.ds((b - half_blocks) * width, width)
        back[0, at, :] = out_t[b].astype(HALF).T
    if split > 1:
        back_copy(0).start()
    for b in range(half_blocks, blocks):
        at = pl.ds((b - half_blocks) * width, width)
        back[1, at, :] = (dq_t[b] * scaling).astype(HALF).T
    if split > 1:
        back_copy(1).start()
    for b in range(half_blocks):
        at = pl.ds(b * width, width)
        heads_out[0, core, at, :] = out_t[b].astype(HALF).T
        heads_out[1, core, at, :] = (dq_t[b] * scaling).astype(HALF).T

    stores = [
        pltpu.make_async_copy(source, target, store_sem.at[i])
        for i, (source, target) in enumerate(
            ((out_ref, out_hbm), (dq_ref, dq_hbm), (dk_ref, dk_hbm), (dv_ref, dv_hbm)))
    ]
    for which, ref in ((0, out_ref), (1, dq_ref)):
        if split > 1:
            back_arrival(which).wait_recv()
        ref[...] = jnp.concatenate(
            [heads_out[which, h].astype(F32).reshape(rows, group, depth) for h in range(split)],
            axis=1).astype(HALF)
        stores[which].start()
    for r, e in others:
        term_arrival(r, e).wait_recv()
    for which, ref in ((0, dk_ref), (1, dv_ref)):
        sums = []
        for h in range(split):
            total = terms[0, h, which].astype(F32)
            for r in range(1, units):
                total = total + terms[r, h, which].astype(F32)
            sums.append(total.reshape(rows, 1, depth))
        ref[...] = jnp.concatenate(sums, axis=1).astype(HALF)
        stores[2 + which].start()
    for store in stores:
        store.wait()
    if split > 1:
        for which in range(2):
            qg_copy(which).wait_send()
            back_copy(which).wait_send()
    for r, e in others:
        for which in range(2):
            kv_copy(which, r, e).wait_send()
        term_copy(r, e).wait_send()


def hand_over(*refs):
    count = (len(refs) - 1) // 2
    copies = [pltpu.make_async_copy(refs[i], refs[count + i], refs[-1].at[i]) for i in range(count)]
    for copy in copies:
        copy.start()
    for copy in copies:
        copy.wait()


def solution(mesh):
    pb_size, ka_size = mesh.shape["pb"], mesh.shape["ka"]

    def on_device(queries, keys, values, out_grad):
        rows, heads, depth = queries.shape
        split = keys.shape[1]
        group = heads // split
        units = pb_size * ka_size // split
        heavy = rows * group
        width = math.gcd(heavy, 512)
        blocks = split * heavy // width
        span = rows * split
        dma, vmem = pltpu.SemaphoreType.DMA, pltpu.VMEM
        in_vmem = pl.BlockSpec(memory_space=pltpu.VMEM)
        in_hbm = pl.BlockSpec(memory_space=pltpu.HBM)
        results = [jax.ShapeDtypeStruct(x.shape, HALF) for x in (queries, queries, keys, values)]
        made = pl.pallas_call(
            functools.partial(kernel, (pb_size, ka_size, split, group, width)),
            out_shape=results,
            in_specs=[in_hbm] * 4,
            out_specs=[in_hbm] * 4,
            scratch_shapes=[
                *[vmem(x.shape, HALF) for x in (keys, values, queries, out_grad)],
                *[vmem(x.shape, HALF) for x in results],
                dma((4,)), dma((4,)),
                vmem((2, split, rows, depth), HALF),
                vmem((units, 2, span, depth), HALF),
                vmem((units, 2, depth, span), HALF),
                vmem((2, split, heavy, depth), HALF),
                vmem((2, split * heavy, depth), HALF),
                vmem((blocks, units, span, width), F32),
                vmem((blocks, units, span, width), F32),
                vmem((blocks, 8, width), F32),
                vmem((blocks, 8, width), F32),
                vmem((blocks, 8, width), F32),
                vmem((blocks, depth, width), F32),
                vmem((blocks, depth, width), F32),
                vmem((2, heavy, depth), HALF),
                vmem((2, split, heavy, depth), HALF),
                vmem((units, 2, span, depth), HALF),
                vmem((units, split, 2, rows, depth), HALF),
                dma((2, units, split)), dma((2, units, split)), dma((2,)), dma((2,)),
                dma((units, split)), dma((units, split)), dma((2,)), dma((2,)),
            ],
            compiler_params=pltpu.CompilerParams(
                collective_id=0, has_side_effects=True, vmem_limit_bytes=58 * 2 ** 20),
            name="attention",
        )(keys, values, queries, out_grad)

        return tuple(pl.pallas_call(
            hand_over,
            out_shape=results,
            in_specs=[in_vmem] * 4,
            out_specs=[in_hbm] * 4,
            scratch_shapes=[dma((4,))],
            compiler_params=pltpu.CompilerParams(vmem_limit_bytes=58 * 2 ** 20),
            name="hand_over",
        )(*made))

    spec = P(("pb", "ka"), "ha", None)
    return jax.shard_map(
        on_device, mesh=mesh, in_specs=(spec,) * 4, out_specs=(spec,) * 4, check_vma=False)
```

```python
import functools
import math

import jax
import jax.numpy as jnp
from jax import lax
from jax.experimental import pallas as pl
from jax.experimental.pallas import tpu as pltpu
from jax.sharding import PartitionSpec as P

MESH = pl.DeviceIdType.MESH
F32 = jnp.float32
HALF = jnp.bfloat16


def fold_rows(x, op):
    return op(x.reshape(x.shape[0] // 8, 8, x.shape[1]), axis=0)


def kernel(dims, k_hbm, v_hbm, q_hbm, g_hbm, heads_out, terms,
           k_ref, v_ref, q_ref, g_ref, kv_stage, kv, kv_t, qg_stage, qg, qg_t,
           scores, grad_probs, prob_half, sums, tops, dots, out_t, dq_t, back, parts,
           load_sem, own_sem, kv_send, kv_recv, qg_send, qg_recv,
           term_send, term_recv, back_send, back_recv):
    pb_size, ka_size, split, group, width = dims
    rows = k_ref.shape[0]
    depth = k_ref.shape[2]
    scaling = depth ** (-0.5)
    exponent = scaling * math.log2(math.e)
    lines = ka_size // split
    units = pb_size * lines
    heavy = rows * group
    blocks = split * heavy // width
    half_blocks = heavy // width

    pb, ka, ha = lax.axis_index("pb"), lax.axis_index("ka"), lax.axis_index("ha")
    core = lax.rem(ka, split)
    line = ka // split

    def core_at(e):
        return lax.rem(core + e, split)

    def device_at(r, e):
        to_pb = lax.rem(pb + r // lines, pb_size)
        return (to_pb, lax.rem(line + r % lines, lines) * split + core_at(e), ha)

    def mirror(r):
        return (pb_size - r // lines) % pb_size * lines + (lines - r % lines) % lines

    def far(r):
        return min(r // lines, pb_size - r // lines) + min(r % lines, lines - r % lines)

    others = [(r, e) for r in range(units) for e in range(split) if (r, e) != (0, 0)]

    near = sorted(others, key=lambda at: far(at[0]))
    siblings = [at for at in near if at[0] == 0]
    farthest = siblings + [at for at in reversed(near) if at[0] != 0]

    def row_slice(which):
        return pl.ds(pl.multiple_of(which * rows, rows), rows)

    def kv_copy(which, r, e):
        return pltpu.make_async_remote_copy(
            src_ref=kv_stage.at[which, core_at(e)],
            dst_ref=kv.at[mirror(r), which, row_slice(core), :],
            send_sem=kv_send.at[which, r, e],
            recv_sem=kv_recv.at[which, mirror(r), (split - e) % split],
            device_id=device_at(r, e), device_id_type=MESH)

    def kv_arrival(which, r, e):
        return pltpu.make_async_remote_copy(
            src_ref=kv_stage.at[which, core],
            dst_ref=kv.at[r, which, row_slice(core_at(e)), :],
            send_sem=kv_send.at[which, r, e], recv_sem=kv_recv.at[which, r, e],
            device_id=device_at(r, e), device_id_type=MESH)

    def qg_copy(which):
        return pltpu.make_async_remote_copy(
            src_ref=qg_stage.at[which, core_at(1)],
            dst_ref=qg.at[which, pl.ds(heavy, heavy), :],
            send_sem=qg_send.at[which], recv_sem=qg_recv.at[which],
            device_id=device_at(0, 1), device_id_type=MESH)

    def term_copy(which, r, e):
        return pltpu.make_async_remote_copy(
            src_ref=parts.at[which, r, row_slice(core_at(e)), :],
            dst_ref=terms.at[mirror(r), core, which],
            send_sem=term_send.at[which, r, e],
            recv_sem=term_recv.at[which, mirror(r), (split - e) % split],
            device_id=device_at(r, e), device_id_type=MESH)

    def term_arrival(which, r, e):
        return pltpu.make_async_remote_copy(
            src_ref=parts.at[which, r, row_slice(core), :],
            dst_ref=terms.at[r, core_at(e), which],
            send_sem=term_send.at[which, r, e], recv_sem=term_recv.at[which, r, e],
            device_id=device_at(r, e), device_id_type=MESH)

    def own_term(which):
        return pltpu.make_async_copy(
            parts.at[which, 0, row_slice(core), :], terms.at[0, core, which], own_sem.at[which])

    def own_heads(which):
        return pltpu.make_async_copy(
            back.at[which, 0], heads_out.at[which, core], own_sem.at[2 + which])

    def back_copy(which):
        return pltpu.make_async_remote_copy(
            src_ref=back.at[which, 1], dst_ref=heads_out.at[which, core],
            send_sem=back_send.at[which], recv_sem=back_recv.at[which],
            device_id=device_at(0, 1), device_id_type=MESH)

    def back_arrival(which):
        return pltpu.make_async_remote_copy(
            src_ref=back.at[which, 1], dst_ref=heads_out.at[which, core_at(1)],
            send_sem=back_send.at[which], recv_sem=back_recv.at[which],
            device_id=device_at(0, 1), device_id_type=MESH)

    loads = [
        pltpu.make_async_copy(source, target, load_sem.at[i])
        for i, (source, target) in enumerate(
            ((k_hbm, k_ref), (v_hbm, v_ref), (q_hbm, q_ref), (g_hbm, g_ref)))
    ]
    for load in loads:
        load.start()
    barrier = pltpu.get_barrier_semaphore()
    for r, e in others:
        pl.semaphore_signal(barrier, inc=1, device_id=device_at(r, e), device_id_type=MESH)

    for which, ref in ((0, k_ref), (1, v_ref)):
        loads[which].wait()
        wide = ref[...].astype(F32)
        for h in range(split):
            kv_stage[which, h] = wide[:, h, :].astype(HALF)
        if which == 0:
            pl.semaphore_wait(barrier, len(others))
        for r, e in farthest:
            kv_copy(which, r, e).start()
        kv[0, which, row_slice(core), :] = kv_stage[which, core]
    for which, ref in ((0, q_ref), (1, g_ref)):
        loads[2 + which].wait()
        wide = ref[...].astype(F32)
        for h in range(split):
            qg_stage[which, h] = (
                wide[:, h * group:(h + 1) * group, :].reshape(heavy, depth).astype(HALF))
        if split > 1:
            qg_copy(which).start()
        qg[which, pl.ds(0, heavy), :] = qg_stage[which, core]

    def block_rows(b):
        return pl.ds(b * width, width)

    def arrive(which, r):
        for e in range(split):
            if (r, e) != (0, 0):
                kv_arrival(which, r, e).wait_recv()

    def turn_block(which, b):
        qg_t[which, b] = qg[which, block_rows(b), :].T

    def score(r, first, last):
        for b in range(first, last):
            s = jnp.dot(kv[r, 0], qg_t[0, b], preferred_element_type=F32)
            scores[b, r] = s
            top = fold_rows(s, jnp.max)
            tops[b] = top if r == 0 else jnp.maximum(tops[b], top)

    def weigh(b):
        top = jnp.max(tops[b], axis=0, keepdims=True) * exponent
        total = jnp.zeros((8, width), F32)
        for r in range(units):
            weights = jnp.exp2(scores[b, r] * exponent - top)
            scores[b, r] = weights
            total = total + fold_rows(weights, jnp.sum)
        return 1.0 / jnp.sum(total, axis=0, keepdims=True)

    def value_terms(b, inverse):
        for r in range(units):
            probs = scores[b, r] * inverse
            half = probs.astype(HALF)
            scores[b, r] = probs
            prob_half[b, r] = half
            dv = jnp.dot(half, qg[1, block_rows(b), :], preferred_element_type=F32)
            sums[r] = dv if b == 0 else sums[r] + dv

    def grade(r, b):
        grad = jnp.dot(kv[r, 1], qg_t[1, b], preferred_element_type=F32)
        grad_probs[b, r] = grad
        dot = fold_rows(scores[b, r] * grad, jnp.sum)
        dots[b] = dot if r == 0 else dots[b] + dot
        out = jnp.dot(kv_t[r, 1], prob_half[b, r], preferred_element_type=F32)
        out_t[b] = out if r == 0 else out_t[b] + out

    def turn(which, r):
        kv_t[r, which] = kv[r, which].T

    def send_terms(which, r):
        for e in range(split):
            if (r, e) != (0, 0):
                term_copy(which, r, e).start()
        if r == 0:
            own_term(which).start()

    def send_heads(which, turned, scale):
        for half in reversed(range(split)):
            for b in range(half_blocks):
                back[which, half, block_rows(b), :] = (
                    (turned[half * half_blocks + b] * scale).astype(HALF).T)
            if half:
                back_copy(which).start()
            else:
                own_heads(which).start()

    for b in range(half_blocks):
        turn_block(0, b)
    arrive(0, 0)
    score(0, 0, half_blocks)
    for b in range(half_blocks):
        turn_block(1, b)
    turn(0, 0)
    if split > 1:
        qg_copy(0).wait_recv()
        for b in range(half_blocks, blocks):
            turn_block(0, b)
        score(0, half_blocks, blocks)
        qg_copy(1).wait_recv()
        for b in range(half_blocks, blocks):
            turn_block(1, b)
    for r in range(1, units):
        arrive(0, r)
        score(r, 0, blocks)
        turn(0, r)
    arrive(1, 0)
    turn(1, 0)
    for b in range(blocks):
        value_terms(b, weigh(b))
        grade(0, b)
    order = sorted(range(units), key=far, reverse=True)
    for r in order:
        parts[1, r] = sums[r].astype(HALF)
        send_terms(1, r)
    for r in range(1, units):
        arrive(1, r)
        turn(1, r)
        for b in range(blocks):
            grade(r, b)
    for b in range(blocks):
        dots[b] = jnp.broadcast_to(jnp.sum(dots[b], axis=0, keepdims=True), (8, width))
    for r in order:
        dk = jnp.zeros((rows * split, depth), F32)
        for b in range(blocks):
            grad_scores = (scores[b, r] * (grad_probs[b, r] - dots[b, 0:1])).astype(HALF)
            dk = dk + jnp.dot(grad_scores, qg[0, block_rows(b), :], preferred_element_type=F32)
            d = jnp.dot(kv_t[r, 0], grad_scores, preferred_element_type=F32)
            dq_t[b] = d if r == order[0] else dq_t[b] + d
        parts[0, r] = (dk * scaling).astype(HALF)
        send_terms(0, r)
        if r == order[0]:
            send_heads(0, out_t, 1.0)
    send_heads(1, dq_t, scaling)

    for which in range(2):
        own_term(which).wait()
        own_heads(which).wait()
        if split > 1:
            back_arrival(which).wait_recv()
            qg_copy(which).wait_send()
            back_copy(which).wait_send()
    for which in range(2):
        for r, e in others:
            kv_copy(which, r, e).wait_send()
            term_copy(which, r, e).wait_send()
    for which in (1, 0):
        for r, e in others:
            term_arrival(which, r, e).wait_recv()


def gather_up(heads_hbm, terms_hbm, out_hbm, dq_hbm, dk_hbm, dv_hbm,
              heads, terms, out_ref, dq_ref, dk_ref, dv_ref, load_sem, store_sem):
    split, heavy, depth = heads.shape[1:]
    units = terms.shape[0]
    rows = terms.shape[3]
    loads = [
        pltpu.make_async_copy(source, target, load_sem.at[i])
        for i, (source, target) in enumerate((
            (heads_hbm.at[0], heads.at[0]), (heads_hbm.at[1], heads.at[1]), (terms_hbm, terms)))
    ]
    stores = [
        pltpu.make_async_copy(source, target, store_sem.at[i])
        for i, (source, target) in enumerate(
            ((out_ref, out_hbm), (dq_ref, dq_hbm), (dk_ref, dk_hbm), (dv_ref, dv_hbm)))
    ]
    for load in loads:
        load.start()
    for which, ref in ((0, out_ref), (1, dq_ref)):
        loads[which].wait()
        ref[...] = jnp.concatenate(
            [heads[which, h].astype(F32).reshape(rows, heavy // rows, depth) for h in range(split)],
            axis=1).astype(HALF)
        stores[which].start()
    loads[2].wait()
    for which, ref in ((0, dk_ref), (1, dv_ref)):
        sums = []
        for h in range(split):
            total = terms[0, h, which].astype(F32)
            for r in range(1, units):
                total = total + terms[r, h, which].astype(F32)
            sums.append(total.reshape(rows, 1, depth))
        ref[...] = jnp.concatenate(sums, axis=1).astype(HALF)
        stores[2 + which].start()
    for store in stores:
        store.wait()


def solution(mesh):
    pb_size, ka_size = mesh.shape["pb"], mesh.shape["ka"]

    def on_device(queries, keys, values, out_grad):
        rows, heads, depth = queries.shape
        split = keys.shape[1]
        group = heads // split
        units = pb_size * ka_size // split
        heavy = rows * group
        width = math.gcd(heavy, 512)
        blocks = split * heavy // width
        span = rows * split
        dma, vmem = pltpu.SemaphoreType.DMA, pltpu.VMEM
        in_hbm = pl.BlockSpec(memory_space=pltpu.HBM)
        shape = jax.ShapeDtypeStruct
        heads_shape = (2, split, heavy, depth)
        terms_shape = (units, split, 2, rows, depth)
        held, summed = pl.pallas_call(
            functools.partial(kernel, (pb_size, ka_size, split, group, width)),
            out_shape=[shape(heads_shape, HALF), shape(terms_shape, HALF)],
            in_specs=[in_hbm] * 4,
            out_specs=[in_hbm] * 2,
            scratch_shapes=[
                *[vmem(x.shape, HALF) for x in (keys, values, queries, out_grad)],
                vmem((2, split, rows, depth), HALF),
                vmem((units, 2, span, depth), HALF),
                vmem((units, 2, depth, span), HALF),
                vmem((2, split, heavy, depth), HALF),
                vmem((2, split * heavy, depth), HALF),
                vmem((2, blocks, depth, width), HALF),
                vmem((blocks, units, span, width), F32),
                vmem((blocks, units, span, width), F32),
                vmem((blocks, units, span, width), HALF),
                vmem((units, span, depth), F32),
                vmem((blocks, 8, width), F32),
                vmem((blocks, 8, width), F32),
                vmem((blocks, depth, width), F32),
                vmem((blocks, depth, width), F32),
                vmem((2, split, heavy, depth), HALF),
                vmem((2, units, span, depth), HALF),
                dma((4,)), dma((4,)),
                dma((2, units, split)), dma((2, units, split)), dma((2,)), dma((2,)),
                dma((2, units, split)), dma((2, units, split)), dma((2,)), dma((2,)),
            ],
            compiler_params=pltpu.CompilerParams(
                collective_id=0, has_side_effects=True, vmem_limit_bytes=58 * 2 ** 20),
            name="attention",
        )(keys, values, queries, out_grad)
        results = [shape(x.shape, HALF) for x in (queries, queries, keys, values)]
        return tuple(pl.pallas_call(
            gather_up,
            out_shape=results,
            in_specs=[in_hbm] * 2,
            out_specs=[in_hbm] * 4,
            scratch_shapes=[
                vmem(heads_shape, HALF), vmem(terms_shape, HALF),
                *[vmem(x.shape, HALF) for x in results],
                dma((3,)), dma((4,)),
            ],
            compiler_params=pltpu.CompilerParams(vmem_limit_bytes=58 * 2 ** 20),
            name="gather_up",
        )(held, summed))

    spec = P(("pb", "ka"), "ha", None)
    return jax.shard_map(
        on_device, mesh=mesh, in_specs=(spec,) * 4, out_specs=(spec,) * 4, check_vma=False)
```

```python
import functools
import math

import jax
import jax.numpy as jnp
from jax import lax
from jax.experimental import pallas as pl
from jax.experimental.pallas import tpu as pltpu
from jax.sharding import PartitionSpec as P

MESH = pl.DeviceIdType.MESH
F32 = jnp.float32
HALF = jnp.bfloat16


def fold_rows(x, op):
    return op(x.reshape(x.shape[0] // 8, 8, x.shape[1]), axis=0)


def kernel(dims, k_hbm, v_hbm, q_hbm, g_hbm, heads_out, terms,
           k_ref, v_ref, q_ref, g_ref, kv_stage, kv, kv_t, qg_stage, qg, qg_t,
           scores, grad_probs, prob_half, sums, tops, inverses, dots, out_t, dq_t, back, parts,
           load_sem, own_sem, kv_send, kv_recv, qg_send, qg_recv,
           term_send, term_recv, back_send, back_recv):
    pb_size, ka_size, split, group, width = dims
    rows = k_ref.shape[0]
    depth = k_ref.shape[2]
    scaling = depth ** (-0.5)
    exponent = scaling * math.log2(math.e)
    lines = ka_size // split
    units = pb_size * lines
    heavy = rows * group
    blocks = split * heavy // width
    half_blocks = heavy // width

    pb, ka, ha = lax.axis_index("pb"), lax.axis_index("ka"), lax.axis_index("ha")
    core = lax.rem(ka, split)
    line = ka // split

    def core_at(e):
        return lax.rem(core + e, split)

    def device_at(r, e):
        to_pb = lax.rem(pb + r // lines, pb_size)
        return (to_pb, lax.rem(line + r % lines, lines) * split + core_at(e), ha)

    def mirror(r):
        return (pb_size - r // lines) % pb_size * lines + (lines - r % lines) % lines

    def far(r):
        return min(r // lines, pb_size - r // lines) + min(r % lines, lines - r % lines)

    others = [(r, e) for r in range(units) for e in range(split) if (r, e) != (0, 0)]

    near = sorted(others, key=lambda at: far(at[0]))
    siblings = [at for at in near if at[0] == 0]
    farthest = siblings + [at for at in reversed(near) if at[0] != 0]

    def row_slice(which):
        return pl.ds(pl.multiple_of(which * rows, rows), rows)

    def kv_copy(which, r, e):
        return pltpu.make_async_remote_copy(
            src_ref=kv_stage.at[which, core_at(e)],
            dst_ref=kv.at[mirror(r), which, row_slice(core), :],
            send_sem=kv_send.at[which, r, e],
            recv_sem=kv_recv.at[which, mirror(r), (split - e) % split],
            device_id=device_at(r, e), device_id_type=MESH)

    def kv_arrival(which, r, e):
        return pltpu.make_async_remote_copy(
            src_ref=kv_stage.at[which, core],
            dst_ref=kv.at[r, which, row_slice(core_at(e)), :],
            send_sem=kv_send.at[which, r, e], recv_sem=kv_recv.at[which, r, e],
            device_id=device_at(r, e), device_id_type=MESH)

    def qg_copy(which):
        return pltpu.make_async_remote_copy(
            src_ref=qg_stage.at[which, core_at(1)],
            dst_ref=qg.at[which, pl.ds(heavy, heavy), :],
            send_sem=qg_send.at[which], recv_sem=qg_recv.at[which],
            device_id=device_at(0, 1), device_id_type=MESH)

    def term_copy(which, r, e):
        return pltpu.make_async_remote_copy(
            src_ref=parts.at[which, r, row_slice(core_at(e)), :],
            dst_ref=terms.at[mirror(r), core, which],
            send_sem=term_send.at[which, r, e],
            recv_sem=term_recv.at[which, mirror(r), (split - e) % split],
            device_id=device_at(r, e), device_id_type=MESH)

    def term_arrival(which, r, e):
        return pltpu.make_async_remote_copy(
            src_ref=parts.at[which, r, row_slice(core), :],
            dst_ref=terms.at[r, core_at(e), which],
            send_sem=term_send.at[which, r, e], recv_sem=term_recv.at[which, r, e],
            device_id=device_at(r, e), device_id_type=MESH)

    def own_term(which):
        return pltpu.make_async_copy(
            parts.at[which, 0, row_slice(core), :], terms.at[0, core, which], own_sem.at[which])

    def own_heads(which):
        return pltpu.make_async_copy(
            back.at[which, 0], heads_out.at[which, core], own_sem.at[2 + which])

    def back_copy(which):
        return pltpu.make_async_remote_copy(
            src_ref=back.at[which, 1], dst_ref=heads_out.at[which, core],
            send_sem=back_send.at[which], recv_sem=back_recv.at[which],
            device_id=device_at(0, 1), device_id_type=MESH)

    def back_arrival(which):
        return pltpu.make_async_remote_copy(
            src_ref=back.at[which, 1], dst_ref=heads_out.at[which, core_at(1)],
            send_sem=back_send.at[which], recv_sem=back_recv.at[which],
            device_id=device_at(0, 1), device_id_type=MESH)

    loads = [
        pltpu.make_async_copy(source, target, load_sem.at[i])
        for i, (source, target) in enumerate(
            ((k_hbm, k_ref), (v_hbm, v_ref), (q_hbm, q_ref), (g_hbm, g_ref)))
    ]
    for load in loads:
        load.start()
    barrier = pltpu.get_barrier_semaphore()
    for r, e in others:
        pl.semaphore_signal(barrier, inc=1, device_id=device_at(r, e), device_id_type=MESH)

    def push_kv(which, ref):
        loads[which].wait()
        wide = ref[...].astype(F32)
        for h in range(split):
            kv_stage[which, h] = wide[:, h, :].astype(HALF)
        if which == 0:
            pl.semaphore_wait(barrier, len(others))
        for r, e in farthest:
            kv_copy(which, r, e).start()
        kv[0, which, row_slice(core), :] = kv_stage[which, core]

    def push_qg(which, ref):
        loads[2 + which].wait()
        wide = ref[...].astype(F32)
        for h in range(split):
            qg_stage[which, h] = (
                wide[:, h * group:(h + 1) * group, :].reshape(heavy, depth).astype(HALF))
        if split > 1:
            qg_copy(which).start()
        qg[which, pl.ds(0, heavy), :] = qg_stage[which, core]

    def block_rows(b):
        return pl.ds(b * width, width)

    def arrive(which, r):
        for e in range(split):
            if (r, e) != (0, 0):
                kv_arrival(which, r, e).wait_recv()

    def turn_block(which, b):
        qg_t[which, b] = qg[which, block_rows(b), :].T

    def score(r, first, last):
        for b in range(first, last):
            s = jnp.dot(kv[r, 0], qg_t[0, b], preferred_element_type=F32)
            scores[b, r] = s
            top = fold_rows(s, jnp.max)
            tops[b] = top if r == 0 else jnp.maximum(tops[b], top)

    def weigh(b):
        top = jnp.max(tops[b], axis=0, keepdims=True) * exponent
        total = jnp.zeros((8, width), F32)
        for r in range(units):
            weights = jnp.exp2(scores[b, r] * exponent - top)
            scores[b, r] = weights
            total = total + fold_rows(weights, jnp.sum)
        inverse = 1.0 / jnp.sum(total, axis=0, keepdims=True)
        inverses[b] = jnp.broadcast_to(inverse, (8, width))
        return inverse

    def value_terms(b, inverse):
        for r in range(units):
            half = (scores[b, r] * inverse).astype(HALF)
            prob_half[b, r] = half
            dv = jnp.dot(half, qg[1, block_rows(b), :], preferred_element_type=F32)
            sums[r] = dv if b == 0 else sums[r] + dv

    def grade(r, b):
        grad = jnp.dot(kv[r, 1], qg_t[1, b], preferred_element_type=F32)
        grad_probs[b, r] = grad
        dot = fold_rows(scores[b, r] * grad, jnp.sum)
        dots[b] = dot if r == 0 else dots[b] + dot
        out = jnp.dot(kv_t[r, 1], prob_half[b, r], preferred_element_type=F32)
        out_t[b] = out if r == 0 else out_t[b] + out

    def turn(which, r):
        kv_t[r, which] = kv[r, which].T

    def send_terms(which, r):
        for e in range(split):
            if (r, e) != (0, 0):
                term_copy(which, r, e).start()
        if r == 0:
            own_term(which).start()

    def send_half(which, half, turned, scale):
        for b in range(half_blocks):
            back[which, half, block_rows(b), :] = (
                (turned[half * half_blocks + b] * scale).astype(HALF).T)
        if half:
            back_copy(which).start()
        else:
            own_heads(which).start()

    push_kv(0, k_ref)
    push_qg(0, q_ref)
    for b in range(half_blocks):
        turn_block(0, b)
    arrive(0, 0)
    score(0, 0, half_blocks)
    push_kv(1, v_ref)
    push_qg(1, g_ref)
    for b in range(half_blocks):
        turn_block(1, b)
    turn(0, 0)
    if split > 1:
        qg_copy(0).wait_recv()
        for b in range(half_blocks, blocks):
            turn_block(0, b)
        score(0, half_blocks, blocks)
        qg_copy(1).wait_recv()
        for b in range(half_blocks, blocks):
            turn_block(1, b)
    for r in range(1, units):
        arrive(0, r)
        score(r, 0, blocks)
        turn(0, r)
    arrive(1, 0)
    turn(1, 0)
    for b in range(blocks):
        value_terms(b, weigh(b))
        grade(0, b)
    order = sorted(range(units), key=far, reverse=True)
    for r in order:
        parts[1, r] = sums[r].astype(HALF)
        send_terms(1, r)
    for r in range(1, units):
        arrive(1, r)
        turn(1, r)
        for b in range(blocks):
            grade(r, b)
    for b in range(blocks):
        dots[b] = jnp.broadcast_to(
            jnp.sum(dots[b], axis=0, keepdims=True) * inverses[b, 0:1], (8, width))
    for r in order:
        dk = jnp.zeros((rows * split, depth), F32)
        for b in reversed(range(blocks)):
            probs = scores[b, r] * inverses[b, 0:1]
            grad_scores = (probs * (grad_probs[b, r] - dots[b, 0:1])).astype(HALF)
            dk = dk + jnp.dot(grad_scores, qg[0, block_rows(b), :], preferred_element_type=F32)
            d = jnp.dot(kv_t[r, 0], grad_scores, preferred_element_type=F32)
            dq_t[b] = d if r == order[0] else dq_t[b] + d
            if r == order[-1] and b == half_blocks and split > 1:
                send_half(1, 1, dq_t, scaling)
        parts[0, r] = (dk * scaling).astype(HALF)
        send_terms(0, r)
        if r == order[0]:
            for half in reversed(range(split)):
                send_half(0, half, out_t, 1.0)
    send_half(1, 0, dq_t, scaling)

    for which in range(2):
        own_term(which).wait()
        own_heads(which).wait()
        if split > 1:
            back_arrival(which).wait_recv()
            qg_copy(which).wait_send()
            back_copy(which).wait_send()
    for which in range(2):
        for r, e in others:
            kv_copy(which, r, e).wait_send()
            term_copy(which, r, e).wait_send()
    for which in (1, 0):
        for r, e in others:
            term_arrival(which, r, e).wait_recv()


def gather_up(heads_hbm, terms_hbm, out_hbm, dq_hbm, dk_hbm, dv_hbm,
              heads, terms, out_ref, dq_ref, dk_ref, dv_ref, load_sem, store_sem):
    split, heavy, depth = heads.shape[1:]
    units = terms.shape[0]
    rows = terms.shape[3]
    loads = [
        pltpu.make_async_copy(source, target, load_sem.at[i])
        for i, (source, target) in enumerate((
            (heads_hbm.at[0], heads.at[0]), (heads_hbm.at[1], heads.at[1]), (terms_hbm, terms)))
    ]
    stores = [
        pltpu.make_async_copy(source, target, store_sem.at[i])
        for i, (source, target) in enumerate(
            ((out_ref, out_hbm), (dq_ref, dq_hbm), (dk_ref, dk_hbm), (dv_ref, dv_hbm)))
    ]
    for load in loads:
        load.start()
    for which, ref in ((0, out_ref), (1, dq_ref)):
        loads[which].wait()
        ref[...] = jnp.concatenate(
            [heads[which, h].astype(F32).reshape(rows, heavy // rows, depth) for h in range(split)],
            axis=1).astype(HALF)
        stores[which].start()
    loads[2].wait()
    for which, ref in ((0, dk_ref), (1, dv_ref)):
        sums = []
        for h in range(split):
            total = terms[0, h, which].astype(F32)
            for r in range(1, units):
                total = total + terms[r, h, which].astype(F32)
            sums.append(total.reshape(rows, 1, depth))
        ref[...] = jnp.concatenate(sums, axis=1).astype(HALF)
        stores[2 + which].start()
    for store in stores:
        store.wait()


def solution(mesh):
    pb_size, ka_size = mesh.shape["pb"], mesh.shape["ka"]

    def on_device(queries, keys, values, out_grad):
        rows, heads, depth = queries.shape
        split = keys.shape[1]
        group = heads // split
        units = pb_size * ka_size // split
        heavy = rows * group
        width = math.gcd(heavy, 512)
        blocks = split * heavy // width
        span = rows * split
        dma, vmem = pltpu.SemaphoreType.DMA, pltpu.VMEM
        in_hbm = pl.BlockSpec(memory_space=pltpu.HBM)
        shape = jax.ShapeDtypeStruct
        heads_shape = (2, split, heavy, depth)
        terms_shape = (units, split, 2, rows, depth)
        held, summed = pl.pallas_call(
            functools.partial(kernel, (pb_size, ka_size, split, group, width)),
            out_shape=[shape(heads_shape, HALF), shape(terms_shape, HALF)],
            in_specs=[in_hbm] * 4,
            out_specs=[in_hbm] * 2,
            scratch_shapes=[
                *[vmem(x.shape, HALF) for x in (keys, values, queries, out_grad)],
                vmem((2, split, rows, depth), HALF),
                vmem((units, 2, span, depth), HALF),
                vmem((units, 2, depth, span), HALF),
                vmem((2, split, heavy, depth), HALF),
                vmem((2, split * heavy, depth), HALF),
                vmem((2, blocks, depth, width), HALF),
                vmem((blocks, units, span, width), F32),
                vmem((blocks, units, span, width), F32),
                vmem((blocks, units, span, width), HALF),
                vmem((units, span, depth), F32),
                vmem((blocks, 8, width), F32),
                vmem((blocks, 8, width), F32),
                vmem((blocks, 8, width), F32),
                vmem((blocks, depth, width), F32),
                vmem((blocks, depth, width), F32),
                vmem((2, split, heavy, depth), HALF),
                vmem((2, units, span, depth), HALF),
                dma((4,)), dma((4,)),
                dma((2, units, split)), dma((2, units, split)), dma((2,)), dma((2,)),
                dma((2, units, split)), dma((2, units, split)), dma((2,)), dma((2,)),
            ],
            compiler_params=pltpu.CompilerParams(
                collective_id=0, has_side_effects=True, vmem_limit_bytes=58 * 2 ** 20),
            name="attention",
        )(keys, values, queries, out_grad)
        results = [shape(x.shape, HALF) for x in (queries, queries, keys, values)]
        return tuple(pl.pallas_call(
            gather_up,
            out_shape=results,
            in_specs=[in_hbm] * 2,
            out_specs=[in_hbm] * 4,
            scratch_shapes=[
                vmem(heads_shape, HALF), vmem(terms_shape, HALF),
                *[vmem(x.shape, HALF) for x in results],
                dma((3,)), dma((4,)),
            ],
            compiler_params=pltpu.CompilerParams(vmem_limit_bytes=58 * 2 ** 20),
            name="gather_up",
        )(held, summed))

    spec = P(("pb", "ka"), "ha", None)
    return jax.shard_map(
        on_device, mesh=mesh, in_specs=(spec,) * 4, out_specs=(spec,) * 4, check_vma=False)
```

```python
import functools
import math

import jax
import jax.numpy as jnp
from jax import lax
from jax.experimental import pallas as pl
from jax.experimental.pallas import tpu as pltpu
from jax.sharding import PartitionSpec as P

MESH = pl.DeviceIdType.MESH
F32 = jnp.float32
HALF = jnp.bfloat16


def fold_rows(x, op):
    return op(x.reshape(x.shape[0] // 8, 8, x.shape[1]), axis=0)


def kernel(dims, k_hbm, v_hbm, q_hbm, g_hbm, heads_out, terms,
           k_ref, v_ref, q_ref, g_ref, kv_stage, kv, kv_t, qg_stage, qg, qg_t,
           scores, grad_probs, prob_half, sums, tops, dots, out_t, dq_t, back, parts,
           load_sem, own_sem, kv_send, kv_recv, qg_send, qg_recv,
           term_send, term_recv, back_send, back_recv):
    pb_size, ka_size, split, group, width = dims
    rows = k_ref.shape[0]
    depth = k_ref.shape[2]
    scaling = depth ** (-0.5)
    exponent = scaling * math.log2(math.e)
    lines = ka_size // split
    units = pb_size * lines
    heavy = rows * group
    blocks = split * heavy // width
    half_blocks = heavy // width
    span = rows * split

    pb, ka, ha = lax.axis_index("pb"), lax.axis_index("ka"), lax.axis_index("ha")
    core = lax.rem(ka, split)
    line = ka // split

    def core_at(e):
        return lax.rem(core + e, split)

    def device_at(r, e):
        to_pb = lax.rem(pb + r // lines, pb_size)
        return (to_pb, lax.rem(line + r % lines, lines) * split + core_at(e), ha)

    def mirror(r):
        return (pb_size - r // lines) % pb_size * lines + (lines - r % lines) % lines

    def far(r):
        return min(r // lines, pb_size - r // lines) + min(r % lines, lines - r % lines)

    others = [(r, e) for r in range(units) for e in range(split) if (r, e) != (0, 0)]

    near = sorted(others, key=lambda at: far(at[0]))
    siblings = [at for at in near if at[0] == 0]
    farthest = siblings + [at for at in reversed(near) if at[0] != 0]

    def row_slice(which):
        return pl.ds(pl.multiple_of(which * rows, rows), rows)

    def kv_copy(which, r, e):
        return pltpu.make_async_remote_copy(
            src_ref=kv_stage.at[which, core_at(e)],
            dst_ref=kv.at[which, mirror(r), row_slice(core), :],
            send_sem=kv_send.at[which, r, e],
            recv_sem=kv_recv.at[which, mirror(r), (split - e) % split],
            device_id=device_at(r, e), device_id_type=MESH)

    def kv_arrival(which, r, e):
        return pltpu.make_async_remote_copy(
            src_ref=kv_stage.at[which, core],
            dst_ref=kv.at[which, r, row_slice(core_at(e)), :],
            send_sem=kv_send.at[which, r, e], recv_sem=kv_recv.at[which, r, e],
            device_id=device_at(r, e), device_id_type=MESH)

    def qg_copy(which):
        return pltpu.make_async_remote_copy(
            src_ref=qg_stage.at[which, core_at(1)],
            dst_ref=qg.at[which, pl.ds(heavy, heavy), :],
            send_sem=qg_send.at[which], recv_sem=qg_recv.at[which],
            device_id=device_at(0, 1), device_id_type=MESH)

    def term_copy(which, r, e):
        return pltpu.make_async_remote_copy(
            src_ref=parts.at[which, r, row_slice(core_at(e)), :],
            dst_ref=terms.at[mirror(r), core, which],
            send_sem=term_send.at[which, r, e],
            recv_sem=term_recv.at[which, mirror(r), (split - e) % split],
            device_id=device_at(r, e), device_id_type=MESH)

    def term_arrival(which, r, e):
        return pltpu.make_async_remote_copy(
            src_ref=parts.at[which, r, row_slice(core), :],
            dst_ref=terms.at[r, core_at(e), which],
            send_sem=term_send.at[which, r, e], recv_sem=term_recv.at[which, r, e],
            device_id=device_at(r, e), device_id_type=MESH)

    def own_term(which):
        return pltpu.make_async_copy(
            parts.at[which, 0, row_slice(core), :], terms.at[0, core, which], own_sem.at[which])

    def own_heads(which):
        return pltpu.make_async_copy(
            back.at[which, 0], heads_out.at[which, core], own_sem.at[2 + which])

    def back_copy(which):
        return pltpu.make_async_remote_copy(
            src_ref=back.at[which, 1], dst_ref=heads_out.at[which, core],
            send_sem=back_send.at[which], recv_sem=back_recv.at[which],
            device_id=device_at(0, 1), device_id_type=MESH)

    def back_arrival(which):
        return pltpu.make_async_remote_copy(
            src_ref=back.at[which, 1], dst_ref=heads_out.at[which, core_at(1)],
            send_sem=back_send.at[which], recv_sem=back_recv.at[which],
            device_id=device_at(0, 1), device_id_type=MESH)

    loads = [
        pltpu.make_async_copy(source, target, load_sem.at[i])
        for i, (source, target) in enumerate(
            ((k_hbm, k_ref), (v_hbm, v_ref), (q_hbm, q_ref), (g_hbm, g_ref)))
    ]
    for load in loads:
        load.start()
    barrier = pltpu.get_barrier_semaphore()
    for r, e in others:
        pl.semaphore_signal(barrier, inc=1, device_id=device_at(r, e), device_id_type=MESH)

    for which, ref in ((0, k_ref), (1, v_ref)):
        loads[which].wait()
        wide = ref[...].astype(F32)
        for h in range(split):
            kv_stage[which, h] = wide[:, h, :].astype(HALF)
        if which == 0:
            pl.semaphore_wait(barrier, len(others))
        for r, e in farthest:
            kv_copy(which, r, e).start()
        kv[which, 0, row_slice(core), :] = kv_stage[which, core]
    for which, ref in ((0, q_ref), (1, g_ref)):
        loads[2 + which].wait()
        wide = ref[...].astype(F32)
        for h in range(split):
            qg_stage[which, h] = (
                wide[:, h * group:(h + 1) * group, :].reshape(heavy, depth).astype(HALF))
        if split > 1:
            qg_copy(which).start()
        qg[which, pl.ds(0, heavy), :] = qg_stage[which, core]

    def block_rows(b):
        return pl.ds(b * width, width)

    def arrive(which, r):
        for e in range(split):
            if (r, e) != (0, 0):
                kv_arrival(which, r, e).wait_recv()

    def turn_block(which, b):
        qg_t[which, b] = qg[which, block_rows(b), :].T

    def score(r, first, last):
        for b in range(first, last):
            s = jnp.dot(kv[0, r], qg_t[0, b], preferred_element_type=F32)
            scores[b, r] = s
            top = fold_rows(s, jnp.max)
            tops[b] = top if r == 0 else jnp.maximum(tops[b], top)

    def weigh(b):
        top = jnp.max(tops[b], axis=0, keepdims=True) * exponent
        total = jnp.zeros((8, width), F32)
        for r in range(units):
            weights = jnp.exp2(scores[b, r] * exponent - top)
            scores[b, r] = weights
            total = total + fold_rows(weights, jnp.sum)
        return 1.0 / jnp.sum(total, axis=0, keepdims=True)

    def value_terms(b, inverse):
        for r in range(units):
            probs = scores[b, r] * inverse
            scores[b, r] = probs
            prob_half[b, pl.ds(r * span, span), :] = probs.astype(HALF)
        dv = jnp.dot(prob_half[b], qg[1, block_rows(b), :], preferred_element_type=F32)
        sums[...] = dv if b == 0 else sums[...] + dv

    def grade(b):
        values = kv[1].reshape(units * span, depth)
        grad = jnp.dot(values, qg_t[1, b], preferred_element_type=F32)
        dot = jnp.zeros((8, width), F32)
        for r in range(units):
            part = grad[r * span:(r + 1) * span]
            grad_probs[b, r] = part
            dot = dot + fold_rows(scores[b, r] * part, jnp.sum)
        dots[b] = jnp.broadcast_to(jnp.sum(dot, axis=0, keepdims=True), (8, width))
        out_t[b] = jnp.dot(kv_t[1], prob_half[b], preferred_element_type=F32)

    def turn(which, r):
        kv_t[which, :, pl.ds(r * span, span)] = kv[which, r].T

    def send_terms(which, r):
        for e in range(split):
            if (r, e) != (0, 0):
                term_copy(which, r, e).start()
        if r == 0:
            own_term(which).start()

    def send_half(which, half, turned, scale):
        for b in range(half_blocks):
            back[which, half, block_rows(b), :] = (
                (turned[half * half_blocks + b] * scale).astype(HALF).T)
        if half:
            back_copy(which).start()
        else:
            own_heads(which).start()

    for b in range(half_blocks):
        turn_block(0, b)
    arrive(0, 0)
    score(0, 0, half_blocks)
    for b in range(half_blocks):
        turn_block(1, b)
    turn(0, 0)
    if split > 1:
        qg_copy(0).wait_recv()
        for b in range(half_blocks, blocks):
            turn_block(0, b)
        score(0, half_blocks, blocks)
        qg_copy(1).wait_recv()
        for b in range(half_blocks, blocks):
            turn_block(1, b)
    for r in range(1, units):
        arrive(0, r)
        score(r, 0, blocks)
        turn(0, r)
    order = sorted(range(units), key=far, reverse=True)

    def take_values(b):
        value_terms(b, weigh(b))
        if b == blocks - 1:
            for r in order:
                parts[1, r] = sums[r * span:(r + 1) * span].astype(HALF)
                send_terms(1, r)

    ahead = (blocks + 1) // 2
    for b in range(ahead):
        take_values(b)
    for r in range(units):
        arrive(1, r)
        turn(1, r)
    for b in range(blocks):
        if b + ahead < blocks:
            take_values(b + ahead)
        grade(b)
    for first in range(0, units, 2):
        pair = order[first:first + 2]
        dk = jnp.zeros((span * len(pair), depth), F32)
        keys_t = jnp.concatenate([kv_t[0, :, r * span:(r + 1) * span] for r in pair], axis=1)
        for b in reversed(range(blocks)):
            grad_scores = jnp.concatenate([
                (scores[b, r] * (grad_probs[b, r] - dots[b, 0:1])).astype(HALF) for r in pair
            ], axis=0)
            dk = dk + jnp.dot(grad_scores, qg[0, block_rows(b), :], preferred_element_type=F32)
            d = jnp.dot(keys_t, grad_scores, preferred_element_type=F32)
            dq_t[b] = d if first == 0 else dq_t[b] + d
            if first + 2 >= units and b == half_blocks and split > 1:
                send_half(1, 1, dq_t, scaling)
        for i, r in enumerate(pair):
            parts[0, r] = (dk[i * span:(i + 1) * span] * scaling).astype(HALF)
            send_terms(0, r)
        if first == 0:
            for half in reversed(range(split)):
                send_half(0, half, out_t, 1.0)
    send_half(1, 0, dq_t, scaling)

    for which in range(2):
        own_term(which).wait()
        own_heads(which).wait()
        if split > 1:
            back_arrival(which).wait_recv()
            qg_copy(which).wait_send()
            back_copy(which).wait_send()
    for which in range(2):
        for r, e in others:
            kv_copy(which, r, e).wait_send()
            term_copy(which, r, e).wait_send()
    for which in (1, 0):
        for r, e in others:
            term_arrival(which, r, e).wait_recv()


def gather_up(heads_hbm, terms_hbm, out_hbm, dq_hbm, dk_hbm, dv_hbm,
              heads, terms, out_ref, dq_ref, dk_ref, dv_ref, load_sem, store_sem):
    split, heavy, depth = heads.shape[1:]
    units = terms.shape[0]
    rows = terms.shape[3]
    loads = [
        pltpu.make_async_copy(source, target, load_sem.at[i])
        for i, (source, target) in enumerate((
            (heads_hbm.at[0], heads.at[0]), (heads_hbm.at[1], heads.at[1]), (terms_hbm, terms)))
    ]
    stores = [
        pltpu.make_async_copy(source, target, store_sem.at[i])
        for i, (source, target) in enumerate(
            ((out_ref, out_hbm), (dq_ref, dq_hbm), (dk_ref, dk_hbm), (dv_ref, dv_hbm)))
    ]
    for load in loads:
        load.start()
    for which, ref in ((0, out_ref), (1, dq_ref)):
        loads[which].wait()
        ref[...] = jnp.concatenate(
            [heads[which, h].astype(F32).reshape(rows, heavy // rows, depth) for h in range(split)],
            axis=1).astype(HALF)
        stores[which].start()
    loads[2].wait()
    for which, ref in ((0, dk_ref), (1, dv_ref)):
        sums = []
        for h in range(split):
            total = terms[0, h, which].astype(F32)
            for r in range(1, units):
                total = total + terms[r, h, which].astype(F32)
            sums.append(total.reshape(rows, 1, depth))
        ref[...] = jnp.concatenate(sums, axis=1).astype(HALF)
        stores[2 + which].start()
    for store in stores:
        store.wait()


def solution(mesh):
    pb_size, ka_size = mesh.shape["pb"], mesh.shape["ka"]

    def on_device(queries, keys, values, out_grad):
        rows, heads, depth = queries.shape
        split = keys.shape[1]
        group = heads // split
        units = pb_size * ka_size // split
        heavy = rows * group
        width = math.gcd(heavy, 512)
        blocks = split * heavy // width
        span = rows * split
        dma, vmem = pltpu.SemaphoreType.DMA, pltpu.VMEM
        in_hbm = pl.BlockSpec(memory_space=pltpu.HBM)
        shape = jax.ShapeDtypeStruct
        heads_shape = (2, split, heavy, depth)
        terms_shape = (units, split, 2, rows, depth)
        held, summed = pl.pallas_call(
            functools.partial(kernel, (pb_size, ka_size, split, group, width)),
            out_shape=[shape(heads_shape, HALF), shape(terms_shape, HALF)],
            in_specs=[in_hbm] * 4,
            out_specs=[in_hbm] * 2,
            scratch_shapes=[
                *[vmem(x.shape, HALF) for x in (keys, values, queries, out_grad)],
                vmem((2, split, rows, depth), HALF),
                vmem((2, units, span, depth), HALF),
                vmem((2, depth, units * span), HALF),
                vmem((2, split, heavy, depth), HALF),
                vmem((2, split * heavy, depth), HALF),
                vmem((2, blocks, depth, width), HALF),
                vmem((blocks, units, span, width), F32),
                vmem((blocks, units, span, width), F32),
                vmem((blocks, units * span, width), HALF),
                vmem((units * span, depth), F32),
                vmem((blocks, 8, width), F32),
                vmem((blocks, 8, width), F32),
                vmem((blocks, depth, width), F32),
                vmem((blocks, depth, width), F32),
                vmem((2, split, heavy, depth), HALF),
                vmem((2, units, span, depth), HALF),
                dma((4,)), dma((4,)),
                dma((2, units, split)), dma((2, units, split)), dma((2,)), dma((2,)),
                dma((2, units, split)), dma((2, units, split)), dma((2,)), dma((2,)),
            ],
            compiler_params=pltpu.CompilerParams(
                collective_id=0, has_side_effects=True, vmem_limit_bytes=58 * 2 ** 20),
            name="attention",
        )(keys, values, queries, out_grad)
        results = [shape(x.shape, HALF) for x in (queries, queries, keys, values)]
        return tuple(pl.pallas_call(
            gather_up,
            out_shape=results,
            in_specs=[in_hbm] * 2,
            out_specs=[in_hbm] * 4,
            scratch_shapes=[
                vmem(heads_shape, HALF), vmem(terms_shape, HALF),
                *[vmem(x.shape, HALF) for x in results],
                dma((3,)), dma((4,)),
            ],
            compiler_params=pltpu.CompilerParams(vmem_limit_bytes=58 * 2 ** 20),
            name="gather_up",
        )(held, summed))

    spec = P(("pb", "ka"), "ha", None)
    return jax.shard_map(
        on_device, mesh=mesh, in_specs=(spec,) * 4, out_specs=(spec,) * 4, check_vma=False)
```

```python
import functools
import math

import jax
import jax.numpy as jnp
from jax import lax
from jax.experimental import pallas as pl
from jax.experimental.pallas import tpu as pltpu
from jax.sharding import PartitionSpec as P

MESH = pl.DeviceIdType.MESH
F32 = jnp.float32
HALF = jnp.bfloat16


def fold_rows(x, op):
    return op(x.reshape(x.shape[0] // 8, 8, x.shape[1]), axis=0)


def kernel(dims, k_hbm, v_hbm, q_hbm, g_hbm, heads_out, terms,
           k_ref, v_ref, q_ref, g_ref, kv_stage, kv, kv_t, qg_stage, qg, qg_t,
           scores, grad_probs, prob_half, sums, tops, dots, out_t, dq_t, back, parts,
           load_sem, own_sem, kv_send, kv_recv, qg_send, qg_recv,
           term_send, term_recv, back_send, back_recv):
    pb_size, ka_size, split, group, width = dims
    rows = k_ref.shape[0]
    depth = k_ref.shape[2]
    scaling = depth ** (-0.5)
    exponent = scaling * math.log2(math.e)
    lines = ka_size // split
    units = pb_size * lines
    heavy = rows * group
    blocks = split * heavy // width
    half_blocks = heavy // width

    pb, ka, ha = lax.axis_index("pb"), lax.axis_index("ka"), lax.axis_index("ha")
    core = lax.rem(ka, split)
    line = ka // split

    def core_at(e):
        return lax.rem(core + e, split)

    def device_at(r, e):
        to_pb = lax.rem(pb + r // lines, pb_size)
        return (to_pb, lax.rem(line + r % lines, lines) * split + core_at(e), ha)

    def mirror(r):
        return (pb_size - r // lines) % pb_size * lines + (lines - r % lines) % lines

    def far(r):
        return min(r // lines, pb_size - r // lines) + min(r % lines, lines - r % lines)

    others = [(r, e) for r in range(units) for e in range(split) if (r, e) != (0, 0)]

    near = sorted(others, key=lambda at: far(at[0]))
    siblings = [at for at in near if at[0] == 0]
    farthest = siblings + [at for at in reversed(near) if at[0] != 0]

    def row_slice(which):
        return pl.ds(pl.multiple_of(which * rows, rows), rows)

    def kv_copy(which, r, e):
        return pltpu.make_async_remote_copy(
            src_ref=kv_stage.at[which, core_at(e)],
            dst_ref=kv.at[mirror(r), which, row_slice(core), :],
            send_sem=kv_send.at[which, r, e],
            recv_sem=kv_recv.at[which, mirror(r), (split - e) % split],
            device_id=device_at(r, e), device_id_type=MESH)

    def kv_arrival(which, r, e):
        return pltpu.make_async_remote_copy(
            src_ref=kv_stage.at[which, core],
            dst_ref=kv.at[r, which, row_slice(core_at(e)), :],
            send_sem=kv_send.at[which, r, e], recv_sem=kv_recv.at[which, r, e],
            device_id=device_at(r, e), device_id_type=MESH)

    def qg_copy(which):
        return pltpu.make_async_remote_copy(
            src_ref=qg_stage.at[which, core_at(1)],
            dst_ref=qg.at[which, pl.ds(heavy, heavy), :],
            send_sem=qg_send.at[which], recv_sem=qg_recv.at[which],
            device_id=device_at(0, 1), device_id_type=MESH)

    def term_copy(which, r, e):
        return pltpu.make_async_remote_copy(
            src_ref=parts.at[which, r, row_slice(core_at(e)), :],
            dst_ref=terms.at[mirror(r), core, which],
            send_sem=term_send.at[which, r, e],
            recv_sem=term_recv.at[which, mirror(r), (split - e) % split],
            device_id=device_at(r, e), device_id_type=MESH)

    def term_arrival(which, r, e):
        return pltpu.make_async_remote_copy(
            src_ref=parts.at[which, r, row_slice(core), :],
            dst_ref=terms.at[r, core_at(e), which],
            send_sem=term_send.at[which, r, e], recv_sem=term_recv.at[which, r, e],
            device_id=device_at(r, e), device_id_type=MESH)

    def own_term(which):
        return pltpu.make_async_copy(
            parts.at[which, 0, row_slice(core), :], terms.at[0, core, which], own_sem.at[which])

    def own_heads(which):
        return pltpu.make_async_copy(
            back.at[which, 0], heads_out.at[which, core], own_sem.at[2 + which])

    def back_copy(which):
        return pltpu.make_async_remote_copy(
            src_ref=back.at[which, 1], dst_ref=heads_out.at[which, core],
            send_sem=back_send.at[which], recv_sem=back_recv.at[which],
            device_id=device_at(0, 1), device_id_type=MESH)

    def back_arrival(which):
        return pltpu.make_async_remote_copy(
            src_ref=back.at[which, 1], dst_ref=heads_out.at[which, core_at(1)],
            send_sem=back_send.at[which], recv_sem=back_recv.at[which],
            device_id=device_at(0, 1), device_id_type=MESH)

    loads = [
        pltpu.make_async_copy(source, target, load_sem.at[i])
        for i, (source, target) in enumerate(
            ((k_hbm, k_ref), (v_hbm, v_ref), (q_hbm, q_ref), (g_hbm, g_ref)))
    ]
    for load in loads:
        load.start()
    barrier = pltpu.get_barrier_semaphore()
    for r, e in others:
        pl.semaphore_signal(barrier, inc=1, device_id=device_at(r, e), device_id_type=MESH)

    for which, ref in ((0, k_ref), (1, v_ref)):
        loads[which].wait()
        wide = ref[...].astype(F32)
        for h in range(split):
            kv_stage[which, h] = wide[:, h, :].astype(HALF)
        if which == 0:
            pl.semaphore_wait(barrier, len(others))
        for r, e in farthest:
            kv_copy(which, r, e).start()
        kv[0, which, row_slice(core), :] = kv_stage[which, core]
    for which, ref in ((0, q_ref), (1, g_ref)):
        loads[2 + which].wait()
        wide = ref[...].astype(F32)
        for h in range(split):
            qg_stage[which, h] = (
                wide[:, h * group:(h + 1) * group, :].reshape(heavy, depth).astype(HALF))
        if split > 1:
            qg_copy(which).start()
        qg[which, pl.ds(0, heavy), :] = qg_stage[which, core]

    def block_rows(b):
        return pl.ds(b * width, width)

    def arrive(which, r):
        for e in range(split):
            if (r, e) != (0, 0):
                kv_arrival(which, r, e).wait_recv()

    def turn_block(which, b):
        qg_t[which, b] = qg[which, block_rows(b), :].T

    def score(r, first, last):
        for b in range(first, last):
            s = jnp.dot(kv[r, 0], qg_t[0, b], preferred_element_type=F32)
            scores[b, r] = s
            top = fold_rows(s, jnp.max)
            tops[b] = top if r == 0 else jnp.maximum(tops[b], top)

    def weigh(b):
        top = jnp.max(tops[b], axis=0, keepdims=True) * exponent
        total = jnp.zeros((8, width), F32)
        for r in range(units):
            weights = jnp.exp2(scores[b, r] * exponent - top)
            scores[b, r] = weights
            total = total + fold_rows(weights, jnp.sum)
        return 1.0 / jnp.sum(total, axis=0, keepdims=True)

    def value_terms(b, inverse):
        for r in range(units):
            probs = scores[b, r] * inverse
            half = probs.astype(HALF)
            scores[b, r] = probs
            prob_half[b, r] = half
            dv = jnp.dot(half, qg[1, block_rows(b), :], preferred_element_type=F32)
            sums[r] = dv if b == 0 else sums[r] + dv

    def grade(r, b):
        grad = jnp.dot(kv[r, 1], qg_t[1, b], preferred_element_type=F32)
        grad_probs[b, r] = grad
        dot = fold_rows(scores[b, r] * grad, jnp.sum)
        dots[b] = dot if r == 0 else dots[b] + dot
        out = jnp.dot(kv_t[r, 1], prob_half[b, r], preferred_element_type=F32)
        out_t[b] = out if r == 0 else out_t[b] + out

    def turn(which, r):
        kv_t[r, which] = kv[r, which].T

    def send_terms(which, r):
        for e in range(split):
            if (r, e) != (0, 0):
                term_copy(which, r, e).start()
        if r == 0:
            own_term(which).start()

    def send_heads(which, turned, scale):
        for half in reversed(range(split)):
            for b in range(half_blocks):
                back[which, half, block_rows(b), :] = (
                    (turned[half * half_blocks + b] * scale).astype(HALF).T)
            if half:
                back_copy(which).start()
            else:
                own_heads(which).start()

    for b in range(half_blocks):
        turn_block(0, b)
    arrive(0, 0)
    score(0, 0, half_blocks)
    for b in range(half_blocks):
        turn_block(1, b)
    turn(0, 0)
    if split > 1:
        qg_copy(0).wait_recv()
        for b in range(half_blocks, blocks):
            turn_block(0, b)
        score(0, half_blocks, blocks)
        qg_copy(1).wait_recv()
        for b in range(half_blocks, blocks):
            turn_block(1, b)
    for r in range(1, units):
        arrive(0, r)
        score(r, 0, blocks)
        turn(0, r)
    arrive(1, 0)
    turn(1, 0)
    for b in range(blocks):
        value_terms(b, weigh(b))
        grade(0, b)
    order = sorted(range(units), key=far, reverse=True)
    for r in order:
        parts[1, r] = sums[r].astype(HALF)
        send_terms(1, r)
    for r in range(1, units):
        arrive(1, r)
        turn(1, r)
        for b in range(blocks):
            grade(r, b)
    for b in range(blocks):
        dots[b] = jnp.broadcast_to(jnp.sum(dots[b], axis=0, keepdims=True), (8, width))
    for r in order:
        dk = jnp.zeros((rows * split, depth), F32)
        for b in range(blocks):
            grad_scores = (scores[b, r] * (grad_probs[b, r] - dots[b, 0:1])).astype(HALF)
            dk = dk + jnp.dot(grad_scores, qg[0, block_rows(b), :], preferred_element_type=F32)
            d = jnp.dot(kv_t[r, 0], grad_scores, preferred_element_type=F32)
            dq_t[b] = d if r == order[0] else dq_t[b] + d
        parts[0, r] = (dk * scaling).astype(HALF)
        send_terms(0, r)
        if r == order[0]:
            send_heads(0, out_t, 1.0)
    send_heads(1, dq_t, scaling)

    for which in range(2):
        own_term(which).wait()
        own_heads(which).wait()
        if split > 1:
            back_arrival(which).wait_recv()
            qg_copy(which).wait_send()
            back_copy(which).wait_send()
    for which in range(2):
        for r, e in others:
            kv_copy(which, r, e).wait_send()
            term_copy(which, r, e).wait_send()
    for which in (1, 0):
        for r, e in others:
            term_arrival(which, r, e).wait_recv()


def gather_up(heads_hbm, terms_hbm, out_hbm, dq_hbm, dk_hbm, dv_hbm,
              heads, terms, out_ref, dq_ref, dk_ref, dv_ref, load_sem, store_sem):
    split, heavy, depth = heads.shape[1:]
    units = terms.shape[0]
    rows = terms.shape[3]
    loads = [
        pltpu.make_async_copy(source, target, load_sem.at[i])
        for i, (source, target) in enumerate((
            (heads_hbm.at[0], heads.at[0]), (heads_hbm.at[1], heads.at[1]), (terms_hbm, terms)))
    ]
    stores = [
        pltpu.make_async_copy(source, target, store_sem.at[i])
        for i, (source, target) in enumerate(
            ((out_ref, out_hbm), (dq_ref, dq_hbm), (dk_ref, dk_hbm), (dv_ref, dv_hbm)))
    ]
    for load in loads:
        load.start()
    for which, ref in ((0, out_ref), (1, dq_ref)):
        loads[which].wait()
        ref[...] = jnp.concatenate(
            [heads[which, h].astype(F32).reshape(rows, heavy // rows, depth) for h in range(split)],
            axis=1).astype(HALF)
        stores[which].start()
    loads[2].wait()
    for which, ref in ((0, dk_ref), (1, dv_ref)):
        sums = []
        for h in range(split):
            total = terms[0, h, which].astype(F32)
            for r in range(1, units):
                total = total + terms[r, h, which].astype(F32)
            sums.append(total.reshape(rows, 1, depth))
        ref[...] = jnp.concatenate(sums, axis=1).astype(HALF)
        stores[2 + which].start()
    for store in stores:
        store.wait()


def solution(mesh):
    pb_size, ka_size = mesh.shape["pb"], mesh.shape["ka"]

    def on_device(queries, keys, values, out_grad):
        rows, heads, depth = queries.shape
        split = keys.shape[1]
        group = heads // split
        units = pb_size * ka_size // split
        heavy = rows * group
        width = math.gcd(heavy, 256)
        blocks = split * heavy // width
        span = rows * split
        dma, vmem = pltpu.SemaphoreType.DMA, pltpu.VMEM
        in_hbm = pl.BlockSpec(memory_space=pltpu.HBM)
        shape = jax.ShapeDtypeStruct
        heads_shape = (2, split, heavy, depth)
        terms_shape = (units, split, 2, rows, depth)
        held, summed = pl.pallas_call(
            functools.partial(kernel, (pb_size, ka_size, split, group, width)),
            out_shape=[shape(heads_shape, HALF), shape(terms_shape, HALF)],
            in_specs=[in_hbm] * 4,
            out_specs=[in_hbm] * 2,
            scratch_shapes=[
                *[vmem(x.shape, HALF) for x in (keys, values, queries, out_grad)],
                vmem((2, split, rows, depth), HALF),
                vmem((units, 2, span, depth), HALF),
                vmem((units, 2, depth, span), HALF),
                vmem((2, split, heavy, depth), HALF),
                vmem((2, split * heavy, depth), HALF),
                vmem((2, blocks, depth, width), HALF),
                vmem((blocks, units, span, width), F32),
                vmem((blocks, units, span, width), F32),
                vmem((blocks, units, span, width), HALF),
                vmem((units, span, depth), F32),
                vmem((blocks, 8, width), F32),
                vmem((blocks, 8, width), F32),
                vmem((blocks, depth, width), F32),
                vmem((blocks, depth, width), F32),
                vmem((2, split, heavy, depth), HALF),
                vmem((2, units, span, depth), HALF),
                dma((4,)), dma((4,)),
                dma((2, units, split)), dma((2, units, split)), dma((2,)), dma((2,)),
                dma((2, units, split)), dma((2, units, split)), dma((2,)), dma((2,)),
            ],
            compiler_params=pltpu.CompilerParams(
                collective_id=0, has_side_effects=True, vmem_limit_bytes=58 * 2 ** 20),
            name="attention",
        )(keys, values, queries, out_grad)
        results = [shape(x.shape, HALF) for x in (queries, queries, keys, values)]
        return tuple(pl.pallas_call(
            gather_up,
            out_shape=results,
            in_specs=[in_hbm] * 2,
            out_specs=[in_hbm] * 4,
            scratch_shapes=[
                vmem(heads_shape, HALF), vmem(terms_shape, HALF),
                *[vmem(x.shape, HALF) for x in results],
                dma((3,)), dma((4,)),
            ],
            compiler_params=pltpu.CompilerParams(vmem_limit_bytes=58 * 2 ** 20),
            name="gather_up",
        )(held, summed))

    spec = P(("pb", "ka"), "ha", None)
    return jax.shard_map(
        on_device, mesh=mesh, in_specs=(spec,) * 4, out_specs=(spec,) * 4, check_vma=False)
```
